32 devices in a mesh: samp: 8 (over y, x, core), tok: 4 (over z).
Axes of the slice: x: 2, y: 2, z: 4, core: 2. Of those that a mesh axis runs over, the one named last changes fastest.
Arguments:
- tokens_in: bfloat16 [16, 768, 768], P('samp', 'tok'), may hold values from -6 to 6
- cotangent: float32 [16, 768, 768], P('samp', 'tok'), may hold values from -6 to 6
- singles: bfloat16 [1, 768, 384], P(None, 'tok'), may hold values from -6 to 6
- noise_table: float32 [256, 384], replicated, may hold values from -6 to 6
- noise_level: int32 [16], P('samp'), may hold values from 0 to 255
- pad_mask: int32 [1, 768], replicated, may hold values from 0 to 1, as said below
- pairwise: bfloat16 [1, 768, 768, 128], P(None, 'tok', 'samp'), may hold values from -6 to 6
- conditioner: bfloat16 [384, 4608], P(None, ('samp', 'tok')), may hold values from -0.3125 to 0.3125
- offsets: bfloat16 [3072], P(('samp', 'tok')), may hold values from -5 to 5
- shifts: bfloat16 [1536], P(('samp', 'tok')), may hold values from -5 to 5
- projector: bfloat16 [768, 3072], P(('samp', 'tok')), may hold values from -0.21875 to 0.21875
- querybias: bfloat16 [768], P(('samp', 'tok')), may hold values from -3 to 3
- combiner: bfloat16 [768, 768], P(('samp', 'tok')), may hold values from -4 to 4
- expander: bfloat16 [768, 3072], P(('samp', 'tok')), may hold values from -0.21875 to 0.21875
- reducer: bfloat16 [1536, 768], P(('samp', 'tok')), may hold values from -0.15625 to 0.15625
- pairhead: bfloat16 [128, 16], replicated, may hold values from -0.5 to 0.5
Outputs:
- mixed: bfloat16 [16, 768, 768], P('samp', 'tok')
- tokens_grad: float32 [16, 768, 768], P('samp', 'tok')
- singles_grad: float32 [1, 768, 384], P(None, 'tok', 'samp')
- pairwise_grad: float32 [1, 768, 768, 128], P(None, 'tok', 'samp')
- noise_grad: float32 [256, 384], replicated
- conditioner_grad: float32 [384, 4608], P(None, ('samp', 'tok'))
- offsets_grad: float32 [3072], P(('samp', 'tok'))
- shifts_grad: float32 [1536], P(('samp', 'tok'))
- projector_grad: float32 [768, 3072], P(('samp', 'tok'))
- querybias_grad: float32 [768], P(('samp', 'tok'))
- combiner_grad: float32 [768, 768], P(('samp', 'tok'))
- expander_grad: float32 [768, 3072], P(('samp', 'tok'))
- reducer_grad: float32 [1536, 768], P(('samp', 'tok'))
- pairhead_grad: float32 [128, 16], replicated
The draws below stay inside these ranges and needn't reach their ends.
Inputs may be any that keep to these rules, and one draw needn't show every extreme that they name: `pad_mask`: in each structure token 0 is real and at least one token is padding; padding may stand anywhere.
All inputs are finite; a program needn't handle non-finite values.
Results may differ from the reference program's by a relative error of at most 0.015.
The reference program's roundings to bfloat16 on the way count: a program that leaves them out, or rounds other values in their place, can miss the bound.
Values may be sent and summed in bfloat16 or wider, within the bound.
No kernel may reach another device: no remote copies, remote signals or barrier semaphores. Data moves between devices by JAX's collectives and lax.ppermute only.
A program may use at most 192 MiB of HBM per device.

```python
import jax
import jax.numpy as jnp
from jax import lax

D = 768
H = 16
CZ = 128
CS = 384
FF = 1536
N = 768
STRUCTS = 1
LEVELS = 256
DH = 48
SAMPLES = 16


def draw_pad_mask(key, part):
    rolls = jax.random.randint(jax.random.fold_in(key, 11), (STRUCTS, N), 0, 8)
    forced = jax.random.randint(jax.random.fold_in(key, 23), (STRUCTS,), 1, N)
    positions = jnp.arange(N, dtype=jnp.int32)
    real = jnp.where(rolls != 0, 1, 0).astype(jnp.int32)
    real = jnp.where(positions[None, :] == forced[:, None], 0, real)
    real = jnp.where(positions[None, :] == 0, 1, real)
    return real.astype(jnp.int32)


def touch_ends(drawn, own_key, smallest, top_value):
    index_at = [jax.random.randint(jax.random.fold_in(own_key, axis), (), 0, length) for axis, length in enumerate(drawn.shape)]
    widest = drawn.shape.index(max(drawn.shape))
    beside = index_at[:widest] + [(index_at[widest] + 1) % drawn.shape[widest]] + index_at[widest + 1:]
    return drawn.at[tuple(index_at)].set(smallest).at[tuple(beside)].set(top_value)


def block_scale(rng, dims, shards, least, largest):
    def one(dim, shards_of):
        draws = jax.random.uniform(jax.random.fold_in(jax.random.fold_in(rng, 6), dim), (shards_of,), jnp.float32, least / len(shards), largest / len(shards))
        return jnp.repeat(jnp.exp(draws), dims[dim] // shards_of).reshape((-1,) + (1,) * (len(dims) - dim - 1))

    factor_of = one(*shards[0])
    for cut in shards[1:]:
        factor_of = factor_of * one(*cut)
    return factor_of


def normal_values(stream_key, dims, spread, most, shards=(), kind=jnp.bfloat16):
    gain = block_scale(stream_key, dims, shards, -0.22, 0.18) if shards else 1.0
    entries = jax.random.normal(stream_key, dims, jnp.float32) * spread * gain
    return jnp.minimum(jnp.maximum(entries, -most), most).astype(kind)


def setup_inputs(seed: int = 0) -> dict:
    streams_of = jax.random.split(jax.random.key(seed), 17)
    tokens_in = normal_values(streams_of[0], (SAMPLES, N, D), 1.0, 6.0, ((0, 8), (1, 4)))
    cotangent = normal_values(streams_of[1], (SAMPLES, N, D), 1.0, 6.0, ((0, 8), (1, 4)), jnp.float32)
    singles = normal_values(streams_of[2], (STRUCTS, N, CS), 1.0, 6.0, ((1, 4),))
    noise_table = normal_values(streams_of[3], (LEVELS, CS), 1.0, 6.0, (), jnp.float32)
    noise_level = touch_ends(jax.random.randint(streams_of[4], (SAMPLES,), 0, LEVELS), jax.random.fold_in(streams_of[4], 1), 0, LEVELS - 1).astype(jnp.int32)
    pad_mask = draw_pad_mask(jax.random.fold_in(streams_of[16], 71), 0)
    pairwise = normal_values(streams_of[6], (STRUCTS, N, N, CZ), 1.0, 6.0, ((1, 4), (2, 8)))
    conditioner = normal_values(streams_of[7], (CS, 6 * D), CS ** -0.5, 0.3125, ((1, 32),))
    offsets = normal_values(streams_of[8], (4 * D,), 1.0, 5.0, ((0, 32),))
    shifts = normal_values(streams_of[9], (2 * D,), 1.0, 5.0, ((0, 32),))
    projector = normal_values(streams_of[10], (D, 4 * D), D ** -0.5, 0.21875, ((0, 32),))
    querybias = normal_values(streams_of[11], (D,), 0.5, 3.0, ((0, 32),))
    combiner = normal_values(streams_of[12], (D, D), 2 ** -0.5, 4.0, ((0, 32),))
    expander = normal_values(streams_of[13], (D, 2 * FF), D ** -0.5, 0.21875, ((0, 32),))
    reducer = normal_values(streams_of[14], (FF, D), FF ** -0.5, 0.15625, ((0, 32),))
    pairhead = normal_values(streams_of[15], (CZ, H), CZ ** -0.5, 0.5)
    return dict(tokens_in=tokens_in, cotangent=cotangent, singles=singles, noise_table=noise_table, noise_level=noise_level, pad_mask=pad_mask, pairwise=pairwise, conditioner=conditioner, offsets=offsets, shifts=shifts, projector=projector, querybias=querybias, combiner=combiner, expander=expander, reducer=reducer, pairhead=pairhead)


@jax.custom_vjp
def low(v):
    return lax.optimization_barrier(v.astype(jnp.bfloat16)).astype(jnp.float32)

@jax.custom_vjp
def low_back(v):
    return v

def low_keep(v):
    return (low(v), None)

def low_pass(kept, grad):
    return (grad,)

def back_keep(v):
    return (v, None)

def back_low(kept, grad):
    return (low(grad),)
low.defvjp(low_keep, low_pass)
low_back.defvjp(back_keep, back_low)
epsilon = 1e-05
highest = lax.Precision.HIGHEST
blocked = 1000000000.0

def normalized_tokens(values):
    center = values - lax.optimization_barrier(jnp.mean(values, axis=-1, keepdims=True))
    return center * lax.rsqrt(lax.optimization_barrier(jnp.mean(center * center, axis=-1, keepdims=True)) + epsilon)

def full_offsets(offsets, shifts):
    scale_parts = jnp.split(offsets, 4)
    shift_parts = jnp.split(shifts, 2)
    return jnp.concatenate([scale_parts[0], shift_parts[0], scale_parts[1], scale_parts[2], shift_parts[1], scale_parts[3]])

def sample_block(tokens_single_sample, structure, level, singles, noise_table, bias_all, mask_all, conditioner, offsets, shifts, projector, querybias, combiner, expander, reducer):
    cond = singles[structure] + noise_table[level][None, :]
    cond_low = low(normalized_tokens(cond))
    adaptive_modulation = low_back(jnp.dot(cond_low, conditioner, precision=highest)) + full_offsets(offsets, shifts)
    before_norm_scale, before_norm_shift, before_gate_input, after_norm_scale, after_norm_shift, after_gate_output = jnp.split(adaptive_modulation, 6, axis=-1)
    before_hidden_units = low(jax.nn.sigmoid(before_norm_scale) * normalized_tokens(tokens_single_sample) + before_norm_shift)
    streams = low_back(jnp.dot(before_hidden_units, projector, precision=highest))
    query = low(streams[:, :D] + querybias).reshape(N, H, DH)
    keys = low(streams[:, D:2 * D]).reshape(N, H, DH)
    values = low(streams[:, 2 * D:3 * D]).reshape(N, H, DH)
    gating = jax.nn.sigmoid(streams[:, 3 * D:])
    product = low_back(jnp.einsum('qhd,khd->hqk', query, keys, precision=highest) * DH ** (-0.5))
    logits = product + jnp.transpose(bias_all[structure], (2, 0, 1)) + ((mask_all[structure] - 1.0) * blocked)[None, None, :]
    shifted = jnp.exp(logits - lax.optimization_barrier(jnp.max(logits, axis=-1, keepdims=True)))
    probs = low(shifted / lax.optimization_barrier(jnp.sum(shifted, axis=-1, keepdims=True)))
    attended = low_back(jnp.einsum('hqk,khd->qhd', probs, values, precision=highest)).reshape(N, D)
    gated = low(gating * attended)
    branch = low_back(jnp.dot(gated, combiner, precision=highest))
    residual = tokens_single_sample + jax.nn.sigmoid(before_gate_input) * branch
    posthidden = low(jax.nn.sigmoid(after_norm_scale) * normalized_tokens(residual) + after_norm_shift)
    upgate = low_back(jnp.dot(posthidden, expander, precision=highest))
    activated = low(jax.nn.silu(upgate[:, :FF]) * upgate[:, FF:])
    trans = low_back(jnp.dot(activated, reducer, precision=highest))
    return residual + jax.nn.sigmoid(after_gate_output) * trans

def forward(tokens, singles, noise_table, pairwise, conditioner, offsets, shifts, projector, querybias, combiner, expander, reducer, pairhead, noise_level, mask_all):
    pair_low = low(normalized_tokens(pairwise))
    bias_all = low(jnp.einsum('sijc,ch->sijh', pair_low, pairhead, precision=highest))

    def one_step(running, inputs):
        tokens_single_sample, sample_id, level = inputs
        result = sample_block(tokens_single_sample, sample_id % STRUCTS, level, singles, noise_table, bias_all, mask_all, conditioner, offsets, shifts, projector, querybias, combiner, expander, reducer)
        return (running, result)
    unused, outputs = lax.scan(jax.checkpoint(one_step), None, (tokens, jnp.arange(SAMPLES, dtype=jnp.int32), noise_level))
    return outputs

def reference(tokens_in, cotangent, singles, noise_table, noise_level, pad_mask, pairwise, conditioner, offsets, shifts, projector, querybias, combiner, expander, reducer, pairhead):
    mask_all = pad_mask.astype(jnp.float32)
    floats = tuple((argument.astype(jnp.float32) for argument in (tokens_in, singles, noise_table, pairwise, conditioner, offsets, shifts, projector, querybias, combiner, expander, reducer, pairhead)))

    def closed(*arrays):
        return forward(*arrays, noise_level, mask_all)
    mixed, pullback = jax.vjp(closed, *floats)
    gradients = pullback(cotangent.astype(jnp.float32))
    return (mixed.astype(jnp.bfloat16), gradients[0], gradients[1], gradients[3], gradients[2], gradients[4], gradients[5], gradients[6], gradients[7], gradients[8], gradients[9], gradients[10], gradients[11], gradients[12])
```

```python
import jax
import jax.numpy as jnp
from jax import lax
from jax.experimental import pallas as pl
from jax.experimental.pallas import tpu as pltpu
from jax.sharding import PartitionSpec as P
DH=48; EPS=1e-5; WIN=256
f32=jnp.float32; bf16=jnp.bfloat16
NT=(((1,),(1,)),((),()))
TN=(((0,),(0,)),((),()))
VL=56*1024*1024

def _window(h, width):
    w = jnp.minimum((h * DH) // 128 * 128, width - WIN)
    w = pl.multiple_of(w, 128)
    lane = lax.broadcasted_iota(jnp.int32, (1, WIN), 1) + w
    return w, (lane >= h * DH) & (lane < h * DH + DH)

def _attn_fwd(q_ref, k_ref, v_ref, bias_ref, mask_ref, p_ref, att_ref):
    h = pl.program_id(0)
    samples, _, width = q_ref.shape
    w, inside = _window(h, width)
    bias = bias_ref[0].astype(f32) + mask_ref[...]
    for b in range(samples):
        q = jnp.where(inside, q_ref[b, :, pl.ds(w, WIN)], 0)
        s = lax.dot_general(q, k_ref[b, :, pl.ds(w, WIN)], NT, preferred_element_type=f32)
        s = s * (DH ** -0.5) + bias
        e = jnp.exp(s - jnp.max(s, axis=1, keepdims=True))
        p = (e * (1.0 / jnp.sum(e, axis=1, keepdims=True))).astype(bf16)
        p_ref[0, b] = p
        o = jnp.dot(p, v_ref[b, :, pl.ds(w, WIN)], preferred_element_type=f32)
        att_ref[b, :, pl.ds(w, WIN)] = jnp.where(inside, o, att_ref[b, :, pl.ds(w, WIN)])

def attn_fwd(q, k, v, bias, mask):
    S, R, D = q.shape; N = k.shape[1]; H = bias.shape[0]
    whole = lambda shape: pl.BlockSpec(shape, lambda h: (0,) * len(shape))
    return pl.pallas_call(
        _attn_fwd, grid=(H,),
        in_specs=[whole((S, R, D)), whole((S, N, D)), whole((S, N, D)),
                  pl.BlockSpec((1, R, N), lambda h: (h, 0, 0)), whole((1, N))],
        out_specs=[pl.BlockSpec((1, S, R, N), lambda h: (h, 0, 0, 0)), whole((S, R, D))],
        out_shape=[jax.ShapeDtypeStruct((H, S, R, N), bf16), jax.ShapeDtypeStruct((S, R, D), f32)],
        compiler_params=pltpu.CompilerParams(vmem_limit_bytes=VL),
        cost_estimate=pl.CostEstimate(flops=4*S*H*R*N*WIN, bytes_accessed=20_000_000, transcendentals=S*H*R*N),
        name="attention",
    )(q, k, v, bias, mask)

def _attn_bwd(p_ref, do_ref, k_ref, v_ref, qt_ref, dot_ref, dq_ref, dkt_ref, dvt_ref, bb_ref):
    h = pl.program_id(0)
    samples, _, width = do_ref.shape
    w, inside = _window(h, width)
    acc = None
    for b in range(samples):
        do = jnp.where(inside, do_ref[b, :, pl.ds(w, WIN)], 0)
        dp = lax.dot_general(do, v_ref[b, :, pl.ds(w, WIN)], NT, preferred_element_type=f32)
        pl_ = p_ref[0, b]
        p = pl_.astype(f32)
        ds = p * (dp - jnp.sum(p * dp, axis=1, keepdims=True))
        acc = ds if acc is None else acc + ds
        dsl = ds.astype(bf16)
        dq = jnp.dot(dsl, k_ref[b, :, pl.ds(w, WIN)], preferred_element_type=f32) * (DH ** -0.5)
        dq_ref[b, :, pl.ds(w, WIN)] = jnp.where(inside, dq, dq_ref[b, :, pl.ds(w, WIN)])
        dkt_ref[b] = (jnp.dot(qt_ref[b], dsl, preferred_element_type=f32) * (DH ** -0.5)).astype(bf16)
        dvt_ref[b] = jnp.dot(dot_ref[b], pl_, preferred_element_type=f32).astype(bf16)
    bb_ref[0] = acc.astype(bb_ref.dtype)

def attn_bwd(p, do, k, v, qt, dot_):
    H, S, R, N = p.shape; D = do.shape[2]
    whole = lambda shape: pl.BlockSpec(shape, lambda h: (0,) * len(shape))
    return pl.pallas_call(
        _attn_bwd, grid=(H,),
        in_specs=[pl.BlockSpec((1, S, R, N), lambda h: (h, 0, 0, 0)), whole((S, R, D)), whole((S, N, D)), whole((S, N, D)),
                  pl.BlockSpec((S, DH, R), lambda h: (0, h, 0)), pl.BlockSpec((S, DH, R), lambda h: (0, h, 0))],
        out_specs=[whole((S, R, D)), pl.BlockSpec((S, DH, N), lambda h: (0, h, 0)), pl.BlockSpec((S, DH, N), lambda h: (0, h, 0)),
                   pl.BlockSpec((1, R, N), lambda h: (h, 0, 0))],
        out_shape=[jax.ShapeDtypeStruct((S, R, D), f32), jax.ShapeDtypeStruct((S, D, N), bf16), jax.ShapeDtypeStruct((S, D, N), bf16),
                   jax.ShapeDtypeStruct((H, R, N), bf16)],
        compiler_params=pltpu.CompilerParams(vmem_limit_bytes=VL),
        cost_estimate=pl.CostEstimate(flops=8*S*H*R*N*WIN, bytes_accessed=30_000_000, transcendentals=0),
        name="attention_back",
    )(p, do, k, v, qt, dot_)

def _normal(x):
    c = x - jnp.mean(x, axis=-1, keepdims=True)
    r = lax.rsqrt(jnp.mean(c * c, axis=-1, keepdims=True) + EPS)
    return c * r, r

def _pair_fwd(x_ref, ph_ref, out_ref, buf):
    n = x_ref.shape[0]
    ph = ph_ref[...]
    for i in range(n):
        nrm, _ = _normal(x_ref[i].astype(f32))
        buf[:, i, :] = lax.dot_general(ph, nrm.astype(bf16), NT, preferred_element_type=f32)
    out_ref[...] = buf[...].astype(bf16)

def pair_fwd(x, pht, blk=16):
    R, C, E = x.shape; H = pht.shape[0]
    return pl.pallas_call(
        _pair_fwd, grid=(R // blk,),
        in_specs=[pl.BlockSpec((blk, C, E), lambda i: (i, 0, 0)), pl.BlockSpec((H, E), lambda i: (0, 0))],
        out_specs=pl.BlockSpec((H, blk, C), lambda i: (0, i, 0)),
        out_shape=jax.ShapeDtypeStruct((H, R, C), bf16),
        scratch_shapes=[pltpu.VMEM((H, blk, C), f32)],
        compiler_params=pltpu.CompilerParams(vmem_limit_bytes=VL),
        cost_estimate=pl.CostEstimate(flops=2*R*C*E*H, bytes_accessed=2*R*C*E, transcendentals=R*C),
        name="pair_bias",
    )(x, pht)

def _split(x):
    hi = x.astype(bf16)
    return jnp.concatenate([hi, (x - hi.astype(f32)).astype(bf16)], axis=0)

def _pair_bwd(x_ref, bb_ref, ph_ref, out_ref, dph_ref):
    n = x_ref.shape[0]
    H = ph_ref.shape[0]
    ph2 = jnp.concatenate([ph_ref[...], ph_ref[...]], axis=0)
    acc = jnp.zeros((2 * H, ph_ref.shape[1]), f32)
    for i in range(n):
        nrm, r = _normal(x_ref[i].astype(f32))
        b2 = _split(bb_ref[i])
        g = lax.dot_general(b2, ph2, TN, preferred_element_type=f32)
        m1 = jnp.mean(g, axis=-1, keepdims=True)
        m2 = jnp.mean(g * nrm, axis=-1, keepdims=True)
        out_ref[i] = r * (g - m1 - nrm * m2)
        acc += jnp.dot(b2, nrm.astype(bf16), preferred_element_type=f32)
    part = acc[:H] + acc[H:]
    @pl.when(pl.program_id(0) == 0)
    def _(): dph_ref[...] = part
    @pl.when(pl.program_id(0) != 0)
    def _(): dph_ref[...] += part

def pair_bwd(x, bb, pht, blk=16):
    R, C, E = x.shape; H = pht.shape[0]
    return pl.pallas_call(
        _pair_bwd, grid=(R // blk,),
        in_specs=[pl.BlockSpec((blk, C, E), lambda i: (i, 0, 0)), pl.BlockSpec((blk, H, C), lambda i: (i, 0, 0)), pl.BlockSpec((H, E), lambda i: (0, 0))],
        out_specs=[pl.BlockSpec((blk, C, E), lambda i: (i, 0, 0)), pl.BlockSpec((H, E), lambda i: (0, 0))],
        out_shape=[jax.ShapeDtypeStruct((R, C, E), f32), jax.ShapeDtypeStruct((H, E), f32)],
        compiler_params=pltpu.CompilerParams(vmem_limit_bytes=VL),
        cost_estimate=pl.CostEstimate(flops=8*R*C*E*H, bytes_accessed=6*R*C*E, transcendentals=R*C),
        name="pair_back",
    )(x, bb, pht)

def normal_rows(x):
    c = x - jnp.mean(x, axis=-1, keepdims=True)
    r = lax.rsqrt(jnp.mean(c * c, axis=-1, keepdims=True) + EPS)
    return c * r, r


def norm_back(n, r, g):
    return r * (g - jnp.mean(g, axis=-1, keepdims=True) - n * jnp.mean(g * n, axis=-1, keepdims=True))


def slope(s):
    return s * (1.0 - s)


def mm(a, b, ca, cb, out=f32):
    return lax.dot_general(a, b, ((ca, cb), ((), ())), preferred_element_type=f32).astype(out)


def hop(x, axis, k):
    n = lax.axis_size(axis)
    return lax.ppermute(x, axis, [(i, i ^ k) for i in range(n)])


def at(x, i):
    return lax.dynamic_index_in_dim(x, i, 0, keepdims=False)


def gather_tok(x):
    n = lax.axis_size("tok")
    if n & (n - 1):
        return lax.all_gather(x, "tok", axis=0)
    t = lax.axis_index("tok")
    out = jnp.zeros((n,) + x.shape, x.dtype)
    out = lax.dynamic_update_slice_in_dim(out, x[None], t, 0)
    for k in range(1, n):
        out = lax.dynamic_update_slice_in_dim(out, hop(x, "tok", k)[None], t ^ k, 0)
    return out


def sum_tok(x):
    n = lax.axis_size("tok")
    if n & (n - 1):
        return lax.psum_scatter(x.astype(bf16), "tok", scatter_dimension=0, tiled=False).astype(f32)
    t = lax.axis_index("tok")
    total = at(x, t).astype(f32)
    for k in range(1, n):
        total = total + hop(at(x, t ^ k).astype(bf16), "tok", k).astype(f32)
    return total


def sum_samp(parts):
    n = lax.axis_size("samp")
    if n != 8:
        whole = jnp.concatenate([p.astype(bf16) for p in parts], axis=-2)
        return lax.psum_scatter(whole, "samp", scatter_dimension=0, tiled=False).astype(f32)
    s = lax.axis_index("samp")
    j, c = s // 2, s % 2

    def half(which):
        picked = [
            lax.dynamic_index_in_dim(p.reshape((n // 2, 2) + p.shape[1:]), which, 1, keepdims=False)
            for p in parts
        ]
        return jnp.concatenate(picked, axis=-2) if len(picked) > 1 else picked[0]

    both = half(c).astype(f32) + hop(half(1 - c).astype(bf16), "samp", 1).astype(f32)
    both = both.astype(bf16)
    total = at(both, j).astype(f32)
    for k in range(1, n // 2):
        total = total + hop(at(both, j ^ k), "samp", 2 * k).astype(f32)
    return total


def per_device(
    tokens_in, cotangent, singles, noise_table, noise_level, pad_mask, pairwise, conditioner,
    offsets, shifts, projector, querybias, combiner, expander, reducer, pairhead,
):
    S, R, D = tokens_in.shape
    C = pairwise.shape[2]
    N = pad_mask.shape[1]
    H = pairhead.shape[1]
    CS = conditioner.shape[0]
    T = lax.axis_size("tok")
    G = lax.axis_size("samp")
    t = lax.axis_index("tok")
    scale_dot = DH ** -0.5

    def blocks(w):
        return [w[:, i * D : (i + 1) * D] for i in range(w.shape[1] // D)]

    cc = conditioner.shape[1]
    cond_t = conditioner.T
    pr = projector.shape[0]
    rr = reducer.shape[0]
    vec = jnp.concatenate([offsets, shifts, querybias])
    vec_row = jnp.zeros((8, D), bf16).at[0, : vec.shape[0]].set(vec)
    cond_rows = jnp.concatenate([cond_t[: cc // 2], cond_t[cc // 2 :]], axis=1)
    first = jnp.concatenate(blocks(projector) + [cond_rows, vec_row], axis=0)
    second = jnp.concatenate(blocks(expander) + [combiner, reducer], axis=0)
    first_all = lax.all_gather(first, ("samp", "tok"), axis=0)
    second_all = lax.all_gather(second, ("samp", "tok"), axis=0)
    W = G * T

    def rows_of(buf, start, count):
        return buf[:, start : start + count].reshape(W * count, D)

    proj_full = jnp.concatenate([rows_of(first_all, i * pr, pr) for i in range(4)], axis=1)
    cond_full = first_all[:, 4 * pr : 4 * pr + cc // 2]
    cond_full = jnp.concatenate([cond_full[:, :, :CS], cond_full[:, :, CS:]], axis=1).reshape(W * cc, CS)
    vecs = first_all[:, 4 * pr + cc // 2].astype(f32)
    no, ns = offsets.shape[0], shifts.shape[0]
    o = jnp.split(vecs[:, :no].reshape(W * no), 4)
    sh = jnp.split(vecs[:, no : no + ns].reshape(W * ns), 2)
    querybias_full = vecs[:, no + ns : no + ns + pr].reshape(W * pr)
    expand_full = jnp.concatenate([rows_of(second_all, i * pr, pr) for i in range(4)], axis=1)
    comb_full = rows_of(second_all, 4 * pr, pr)
    reduce_full = rows_of(second_all, 5 * pr, rr)

    pht = pairhead.T
    piece = pair_fwd(pairwise[0], pht)
    bias_all = jnp.transpose(lax.all_gather(piece, "samp", axis=0), (1, 2, 0, 3)).reshape(H, R, N)
    mask_add = (pad_mask.astype(f32) - 1.0) * 1e9

    singles_rows = jnp.concatenate([singles[0, : R // 2], singles[0, R // 2 :]], axis=1)
    mine = jnp.concatenate([tokens_in.reshape(S * R, D), singles_rows], axis=0)
    every = gather_tok(mine)
    tokens_all = every[:, : S * R].reshape(T, S, R, D).transpose(1, 0, 2, 3).reshape(S, N, D)
    halves = every[:, S * R :]
    singles_all = jnp.concatenate([halves[:, :, :CS], halves[:, :, CS:]], axis=1).reshape(N, CS)

    noise_rows = jnp.stack([at(noise_table, noise_level[b]) for b in range(S)])
    cond_norm_all, cond_inv_all = normal_rows(singles_all.astype(f32)[None] + noise_rows[:, None])
    cond_low_all = cond_norm_all.astype(bf16)

    def own(x):
        return lax.dynamic_slice_in_dim(x, t * R, R, 1)

    adapt_pre = mm(cond_low_all, cond_full[: 2 * D], (2,), (1,)) + jnp.concatenate([o[0], sh[0]])
    cond_norm, cond_inv = normal_rows(singles.astype(f32) + noise_rows[:, None])
    cond_low = cond_norm.astype(bf16)
    adapt_own = mm(cond_low, cond_full[2 * D :], (2,), (1,)) + jnp.concatenate([o[1], o[2], sh[1], o[3]])
    pregate, postscale, postshift, postgate = jnp.split(adapt_own, 4, axis=-1)

    token_norm_all, token_inv_all = normal_rows(tokens_all.astype(f32))
    gain_all = jax.nn.sigmoid(adapt_pre[..., :D])
    pre_all = (gain_all * token_norm_all + adapt_pre[..., D:]).astype(bf16)
    pre = own(pre_all)
    keys = mm(pre_all, proj_full[:, D : 2 * D], (2,), (0,), bf16)
    values = mm(pre_all, proj_full[:, 2 * D : 3 * D], (2,), (0,), bf16)
    query = (mm(pre, proj_full[:, :D], (2,), (0,)) + querybias_full).astype(bf16)
    gating = jax.nn.sigmoid(mm(pre, proj_full[:, 3 * D :], (2,), (0,)))

    probs, attended = attn_fwd(query, keys, values, bias_all, mask_add)

    tokens = tokens_in.astype(f32)
    gated = (gating * attended).astype(bf16)
    branch = mm(gated, comb_full, (2,), (0,))
    pregate_sig = jax.nn.sigmoid(pregate)
    residual = tokens + pregate_sig * branch
    post_norm, post_inv = normal_rows(residual)
    post_gain = jax.nn.sigmoid(postscale)
    posthidden = (post_gain * post_norm + postshift).astype(bf16)
    upgate = mm(posthidden, expand_full, (2,), (0,))
    FF = upgate.shape[-1] // 2
    preact, upper = upgate[..., :FF], upgate[..., FF:]
    preact_sig = jax.nn.sigmoid(preact)
    swished = preact * preact_sig
    activated = (swished * upper).astype(bf16)
    trans = mm(activated, reduce_full, (2,), (0,))
    postgate_sig = jax.nn.sigmoid(postgate)
    mixed = (residual + postgate_sig * trans).astype(bf16)

    def owned(grad):
        return [
            g.reshape(G, T, g.shape[0] // W, D)
            for g in (grad[:, i * D : (i + 1) * D] for i in range(grad.shape[1] // D))
        ]

    trans_back = (postgate_sig * cotangent).astype(bf16)
    postgate_back = cotangent * trans * slope(postgate_sig)
    reducer_part = mm(activated, trans_back, (0, 1), (0, 1), bf16)
    act_back = mm(trans_back, reduce_full, (2,), (1,))
    up_back = jnp.concatenate(
        [act_back * upper * preact_sig * (1.0 + preact * (1.0 - preact_sig)), act_back * swished], axis=-1
    ).astype(bf16)
    expander_part = mm(posthidden, up_back, (0, 1), (0, 1), bf16)
    posthidden_back = mm(up_back, expand_full, (2,), (1,))
    postscale_back = posthidden_back * post_norm * slope(post_gain)
    residual_back = cotangent + norm_back(post_norm, post_inv, posthidden_back * post_gain)
    branch_back = (pregate_sig * residual_back).astype(bf16)
    pregate_back = residual_back * branch * slope(pregate_sig)
    combiner_part = mm(gated, branch_back, (0, 1), (0, 1), bf16)
    second_sum = sum_tok(
        sum_samp(
            [
                p.reshape(G, -1, D)
                for p in [jnp.concatenate(owned(expander_part) + owned(combiner_part) + owned(reducer_part), axis=2)]
            ]
        ).reshape(T, -1, D)
    )

    gated_back = mm(branch_back, comb_full, (2,), (1,))
    attended_back = (gating * gated_back).astype(bf16)
    gating_back = attended * gated_back * slope(gating)
    query_back, keys_back_t, values_back_t, bias_back = attn_bwd(
        probs, attended_back, keys, values, query.transpose(0, 2, 1), attended_back.transpose(0, 2, 1)
    )
    bias_sum = sum_samp([bias_back.reshape(H * R, G, C).transpose(1, 0, 2)]).reshape(H, R, C)
    pair_grad, pairhead_part = pair_bwd(pairwise[0], bias_sum.transpose(1, 0, 2), pht)

    query_low = query_back.astype(bf16)
    gating_low = gating_back.astype(bf16)
    pre_back_all = mm(keys_back_t, proj_full[:, D : 2 * D], (1,), (1,)) + mm(
        values_back_t, proj_full[:, 2 * D : 3 * D], (1,), (1,)
    )
    pre_back = sum_tok(pre_back_all.astype(bf16).reshape(S, T, R, D).transpose(1, 0, 2, 3))
    pre_back = pre_back + mm(query_low, proj_full[:, :D], (2,), (1,)) + mm(gating_low, proj_full[:, 3 * D :], (2,), (1,))
    projector_parts = [
        mm(pre, query_low, (0, 1), (0, 1), bf16),
        mm(pre_all, keys_back_t, (0, 1), (0, 2), bf16),
        mm(pre_all, values_back_t, (0, 1), (0, 2), bf16),
        mm(pre, gating_low, (0, 1), (0, 1), bf16),
    ]
    token_norm, token_inv = normal_rows(tokens)
    gain = jax.nn.sigmoid(own(adapt_pre[..., :D]))
    prescale_back = pre_back * token_norm * slope(gain)
    tokens_grad = residual_back + norm_back(token_norm, token_inv, pre_back * gain)
    adapt_back = jnp.concatenate(
        [prescale_back, pre_back, pregate_back, postscale_back, posthidden_back, postgate_back], axis=-1
    )
    sums = jnp.split(jnp.sum(adapt_back, axis=(0, 1)), 6)
    offsets_part = jnp.concatenate([sums[0], sums[2], sums[3], sums[5]])
    shifts_part = jnp.concatenate([sums[1], sums[4]])
    querybias_part = jnp.sum(query_back, axis=(0, 1))
    adapt_low = adapt_back.astype(bf16)
    cond_part = mm(adapt_low, cond_low, (0, 1), (0, 1), bf16).reshape(G, T, cc, CS)
    cond_part = jnp.concatenate([cond_part[:, :, : cc // 2], cond_part[:, :, cc // 2 :]], axis=-1)
    vec_part = jnp.concatenate(
        [offsets_part.reshape(G, T, no), shifts_part.reshape(G, T, ns), querybias_part.reshape(G, T, pr)], axis=-1
    )
    vec_part = jnp.zeros((G, T, 8, D), bf16).at[:, :, 0, : vec.shape[0]].set(vec_part.astype(bf16))
    first_part = jnp.concatenate([x for p in projector_parts for x in owned(p)] + [cond_part, vec_part], axis=2)
    first_sum = sum_tok(sum_samp([first_part.reshape(G, -1, D)]).reshape(T, -1, D))

    cond_grad = norm_back(cond_norm, cond_inv, mm(adapt_low, cond_full, (2,), (0,)))
    cs = CS // G
    singles_grad = sum_samp([jnp.sum(cond_grad, axis=0).reshape(R, G, cs).transpose(1, 2, 0)]).T[None]
    levels = jnp.arange(noise_table.shape[0], dtype=jnp.int32)
    level_hot = (noise_level[:, None] == levels[None, :]).astype(f32)
    noise_part = jnp.dot(level_hot.T, jnp.sum(cond_grad, axis=1), precision=lax.Precision.HIGHEST)
    noise_grad, pairhead_grad = lax.psum((noise_part, pairhead_part), ("samp", "tok"))

    def unblocks(x):
        return jnp.concatenate([x[i * pr : (i + 1) * pr] for i in range(4)], axis=1)

    projector_grad = unblocks(first_sum)
    cond_out = first_sum[4 * pr : 4 * pr + cc // 2]
    conditioner_grad = jnp.concatenate([cond_out[:, :CS], cond_out[:, CS:]], axis=0).T
    vec_out = first_sum[4 * pr + cc // 2]
    expander_grad = unblocks(second_sum)
    combiner_grad = second_sum[4 * pr : 5 * pr]
    reducer_grad = second_sum[5 * pr :]
    return (
        mixed,
        tokens_grad,
        singles_grad,
        pair_grad[None],
        noise_grad,
        conditioner_grad,
        vec_out[:no],
        vec_out[no : no + ns],
        projector_grad,
        vec_out[no + ns : no + ns + pr],
        combiner_grad,
        expander_grad,
        reducer_grad,
        pairhead_grad.T,
    )


def solution(mesh):
    shard = ("samp", "tok")
    in_specs = (
        P("samp", "tok", None), P("samp", "tok", None), P(None, "tok", None), P(), P("samp"), P(),
        P(None, "tok", "samp", None), P(None, shard), P(shard), P(shard), P(shard, None), P(shard),
        P(shard, None), P(shard, None), P(shard, None), P(),
    )
    out_specs = (
        P("samp", "tok", None), P("samp", "tok", None), P(None, "tok", "samp"), P(None, "tok", "samp", None), P(),
        P(None, shard), P(shard), P(shard), P(shard, None), P(shard), P(shard, None), P(shard, None),
        P(shard, None), P(),
    )
    return jax.shard_map(per_device, mesh=mesh, in_specs=in_specs, out_specs=out_specs, check_vma=False)
```

```python
import jax
import jax.numpy as jnp
from jax import lax
from jax.experimental import pallas as pl
from jax.experimental.pallas import tpu as pltpu
from jax.sharding import PartitionSpec as P

DH = 48
EPS = 1e-5
WIN = 256
VMEM_BYTES = 56 * 1024 * 1024
f32 = jnp.float32
bf16 = jnp.bfloat16
COST = pl.CostEstimate(flops=1024, bytes_accessed=1024, transcendentals=0)
NT = (((1,), (1,)), ((), ()))
TN = (((0,), (0,)), ((), ()))


def params():
    return pltpu.CompilerParams(vmem_limit_bytes=VMEM_BYTES)


def window(h, width):
    w = pl.multiple_of(jnp.minimum((h * DH) // 128 * 128, width - WIN), 128)
    lane = lax.broadcasted_iota(jnp.int32, (1, WIN), 1) + w
    return w, (lane >= h * DH) & (lane < h * DH + DH)


def attention_body(q_ref, k_ref, v_ref, bias_ref, mask_ref, p_ref, att_ref):
    samples, _, width = q_ref.shape
    w, inside = window(pl.program_id(0), width)
    bias = bias_ref[0].astype(f32) + mask_ref[...]
    for b in range(samples):
        q = jnp.where(inside, q_ref[b, :, pl.ds(w, WIN)], 0)
        s = lax.dot_general(q, k_ref[b, :, pl.ds(w, WIN)], NT, preferred_element_type=f32)
        s = s * (DH ** -0.5) + bias
        e = jnp.exp(s - jnp.max(s, axis=1, keepdims=True))
        p = (e * (1.0 / jnp.sum(e, axis=1, keepdims=True))).astype(bf16)
        p_ref[0, b] = p
        o = jnp.dot(p, v_ref[b, :, pl.ds(w, WIN)], preferred_element_type=f32)
        att_ref[b, :, pl.ds(w, WIN)] = jnp.where(inside, o, att_ref[b, :, pl.ds(w, WIN)])


def attention(q, kv, bias, mask):
    S, R, D = q.shape
    N, H = kv.shape[1], bias.shape[0]

    def whole(*shape):
        return pl.BlockSpec(shape, lambda h: (0,) * len(shape))

    return pl.pallas_call(
        attention_body,
        grid=(H,),
        in_specs=[
            whole(S, R, D),
            whole(S, N, D),
            pl.BlockSpec((S, N, D), lambda h: (0, 0, 1)),
            pl.BlockSpec((1, R, N), lambda h: (h, 0, 0)),
            whole(1, N),
        ],
        out_specs=[pl.BlockSpec((1, S, R, N), lambda h: (h, 0, 0, 0)), whole(S, R, D)],
        out_shape=[jax.ShapeDtypeStruct((H, S, R, N), bf16), jax.ShapeDtypeStruct((S, R, D), f32)],
        compiler_params=params(),
        cost_estimate=COST,
        name="attention",
    )(q, kv, kv, bias, mask)


def attention_back_body(fold, me_ref, p_ref, do_ref, k_ref, v_ref, q_ref, dq_ref, dkv_ref, *rest):
    *bb_refs, qt, dot_ = rest
    samples, rows, width = do_ref.shape
    h = pl.program_id(0)
    w, inside = window(h, width)

    @pl.when(h == 0)
    def _():
        for b in range(samples):
            qt[b] = q_ref[b].astype(f32).T.astype(bf16)
            dot_[b] = do_ref[b].astype(f32).T.astype(bf16)

    own = pl.ds(pl.multiple_of(h * DH, 16), DH)
    acc = None
    for b in range(samples):
        do = jnp.where(inside, do_ref[b, :, pl.ds(w, WIN)], 0)
        dp = lax.dot_general(do, v_ref[b, :, pl.ds(w, WIN)], NT, preferred_element_type=f32)
        p_low = p_ref[0, b]
        p = p_low.astype(f32)
        ds = p * (dp - jnp.sum(p * dp, axis=1, keepdims=True))
        acc = ds if acc is None else acc + ds
        low = ds.astype(bf16)
        dq = jnp.dot(low, k_ref[b, :, pl.ds(w, WIN)], preferred_element_type=f32) * (DH ** -0.5)
        dq_ref[b, :, pl.ds(w, WIN)] = jnp.where(inside, dq, dq_ref[b, :, pl.ds(w, WIN)])
        dk = jnp.dot(qt[b, own, :], low, preferred_element_type=f32) * (DH ** -0.5)
        dkv_ref[b, 0] = dk.astype(bf16)
        dkv_ref[b, 1] = jnp.dot(dot_[b, own, :], p_low, preferred_element_type=f32).astype(bf16)
    if fold == 1:
        bb_refs[0][0] = acc.astype(bf16)
    else:
        kept_ref, given_ref = bb_refs
        count, _, part, lanes = kept_ref.shape
        c = lanes // fold
        odd = me_ref[0] % 2 == 1

        def piece(s):
            return jnp.concatenate(
                [acc[i * part : (i + 1) * part, s * c : (s + 1) * c] for i in range(fold)], axis=1
            )

        for j in range(count):
            first, second = piece(2 * j), piece(2 * j + 1)
            kept_ref[j, 0] = jnp.where(odd, second, first).astype(bf16)
            given_ref[j, 0] = jnp.where(odd, first, second).astype(bf16)


def attention_back(me, p, do, kv, q, first, fold, groups):
    H, S, R, N = p.shape
    D = do.shape[2]

    def whole(*shape):
        return pl.BlockSpec(shape, lambda h, m: (0,) * len(shape))

    if fold == 1:
        bb_specs, bb_shapes = [pl.BlockSpec((1, R, N), lambda h, m: (h, 0, 0))], [(H, R, N)]
    else:
        tail = (R // fold, fold * (N // groups))
        bb_specs = [pl.BlockSpec((groups // 2, 1) + tail, lambda h, m: (0, h, 0, 0))] * 2
        bb_shapes = [(groups // 2, H) + tail] * 2

    def body(me_ref, p_ref, do_ref, k_ref, v_ref, q_ref, _, *refs):
        attention_back_body(fold, me_ref, p_ref, do_ref, k_ref, v_ref, q_ref, *refs)

    return pl.pallas_call(
        body,
        grid_spec=pltpu.PrefetchScalarGridSpec(
            num_scalar_prefetch=1,
            grid=(H,),
            in_specs=[
                pl.BlockSpec((1, S, R, N), lambda h, m: (h, 0, 0, 0)),
                whole(S, R, D),
                whole(S, N, D),
                pl.BlockSpec((S, N, D), lambda h, m: (0, 0, 1)),
                whole(S, R, D),
                pl.BlockSpec(memory_space=pl.ANY),
            ],
            out_specs=[whole(S, R, D), pl.BlockSpec((S, 2, DH, N), lambda h, m: (0, 0, h, 0))] + bb_specs,
            scratch_shapes=[pltpu.VMEM((S, D, R), bf16), pltpu.VMEM((S, D, R), bf16)],
        ),
        out_shape=[
            jax.ShapeDtypeStruct((S, R, D), f32),
            jax.ShapeDtypeStruct((S, 2, D, N), bf16),
        ]
        + [jax.ShapeDtypeStruct(shape, bf16) for shape in bb_shapes],
        compiler_params=params(),
        cost_estimate=COST,
        name="attention_back",
    )(me, p, do, kv, kv, q, first)


def normal_rows(x):
    c = x - jnp.mean(x, axis=-1, keepdims=True)
    r = lax.rsqrt(jnp.mean(c * c, axis=-1, keepdims=True) + EPS)
    return c * r, r


def split(x):
    hi = x.astype(bf16)
    return hi, (x - hi.astype(f32)).astype(bf16)


def lane_mean(x):
    ones = jnp.full((x.shape[1], x.shape[1]), 1.0, bf16)
    hi, lo = split(x)
    total = jnp.dot(hi, ones, preferred_element_type=f32) + jnp.dot(lo, ones, preferred_element_type=f32)
    return total * (1.0 / x.shape[1])


def pair_bias_body(x_ref, ph_ref, out_ref, buf):
    fold, n, C, E = x_ref.shape
    ph = ph_ref[...]
    for i in range(n):
        x = x_ref[:, i].reshape(fold * C, E) if fold > 1 else x_ref[0, i]
        nrm, _ = normal_rows(x.astype(f32))
        buf[:, i, :] = lax.dot_general(ph, nrm.astype(bf16), NT, preferred_element_type=f32)
    out_ref[...] = buf[...].astype(bf16)


def pair_bias(x, pht, fold):
    R, C, E = x.shape
    H = pht.shape[0]
    rows = R // fold
    blk = 16
    return pl.pallas_call(
        pair_bias_body,
        grid=(rows // blk,),
        in_specs=[
            pl.BlockSpec((fold, blk, C, E), lambda i: (0, i, 0, 0)), pl.BlockSpec((H, E), lambda i: (0, 0)),
        ],
        out_specs=pl.BlockSpec((H, blk, fold * C), lambda i: (0, i, 0)),
        out_shape=jax.ShapeDtypeStruct((H, rows, fold * C), bf16),
        scratch_shapes=[pltpu.VMEM((H, blk, fold * C), f32)],
        compiler_params=params(),
        cost_estimate=COST,
        name="pair_bias",
    )(x.reshape(fold, rows, C, E), pht)


def pair_back_body(x_ref, bb_ref, ph_ref, out_ref, dph_ref):
    fold, n, C, E = x_ref.shape
    H = ph_ref.shape[0]
    ph = ph_ref[...].astype(f32)
    ph_hi, ph_lo = split(ph - jnp.mean(ph, axis=-1, keepdims=True))
    ph4 = jnp.concatenate([ph_hi, ph_lo, ph_hi, ph_lo], axis=0)
    acc = jnp.zeros((2 * H, E), f32)
    for i in range(n):
        x = x_ref[:, i].reshape(fold * C, E) if fold > 1 else x_ref[0, i]
        ones = jnp.full((E, E), 1.0, bf16)
        c = x.astype(f32) - jnp.dot(x, ones, preferred_element_type=f32) * (1.0 / E)
        r = lax.rsqrt(lane_mean(c * c) + EPS)
        nrm = c * r
        hi, lo = split(bb_ref[i])
        g = lax.dot_general(
            jnp.concatenate([hi, hi, lo, lo], axis=0), ph4, TN, preferred_element_type=f32
        )
        grad = r * (g - nrm * jnp.mean(g * nrm, axis=-1, keepdims=True))
        if fold > 1:
            out_ref[:, i] = grad.reshape(fold, C, E)
        else:
            out_ref[0, i] = grad
        acc += jnp.dot(jnp.concatenate([hi, lo], axis=0), nrm.astype(bf16), preferred_element_type=f32)
    part = acc[:H] + acc[H:]

    @pl.when(pl.program_id(0) == 0)
    def _():
        dph_ref[...] = part

    @pl.when(pl.program_id(0) != 0)
    def _():
        dph_ref[...] += part


def pair_back(x, bb, pht, fold):
    R, C, E = x.shape
    H = pht.shape[0]
    rows = R // fold
    blk = 8
    grad, dph = pl.pallas_call(
        pair_back_body,
        grid=(rows // blk,),
        in_specs=[
            pl.BlockSpec((fold, blk, C, E), lambda i: (0, i, 0, 0)),
            pl.BlockSpec((blk, H, fold * C), lambda i: (i, 0, 0)),
            pl.BlockSpec((H, E), lambda i: (0, 0)),
        ],
        out_specs=[pl.BlockSpec((fold, blk, C, E), lambda i: (0, i, 0, 0)), pl.BlockSpec((H, E), lambda i: (0, 0))],
        out_shape=[jax.ShapeDtypeStruct((fold, rows, C, E), f32), jax.ShapeDtypeStruct((H, E), f32)],
        compiler_params=params(),
        cost_estimate=COST,
        name="pair_back",
    )(x.reshape(fold, rows, C, E), bb, pht)
    return grad.reshape(R, C, E), dph


def lay_bias_body(me_ref, *refs):
    pieces, (out_ref, slots, sems) = refs[:-3], refs[-3:]
    h = pl.program_id(0)
    part, lanes = slots.shape[2:]
    fold = out_ref.shape[1] // part
    c = lanes // fold

    @pl.when(h == 0)
    def _():
        copies = [
            pltpu.make_async_copy(p, slots.at[jnp.bitwise_xor(me_ref[0], k)], sems.at[k]) for k, p in enumerate(pieces)
        ]
        for copy in copies:
            copy.start()
        for copy in copies:
            copy.wait()

    laid = [slots[s, h].astype(f32) for s in range(len(pieces))]
    for i in range(fold):
        out_ref[0, i * part : (i + 1) * part, :] = jnp.concatenate(
            [p[:, i * c : (i + 1) * c] for p in laid], axis=1
        ).astype(bf16)


def lay_bias(me, pieces, rows):
    H, part, lanes = pieces[0].shape
    count = len(pieces)
    keys = count * lanes // (rows // part)
    return pl.pallas_call(
        lay_bias_body,
        grid_spec=pltpu.PrefetchScalarGridSpec(
            num_scalar_prefetch=1,
            grid=(H,),
            in_specs=[pl.BlockSpec(memory_space=pl.ANY)] * count,
            out_specs=pl.BlockSpec((1, rows, keys), lambda h, s: (h, 0, 0)),
            scratch_shapes=[pltpu.VMEM((count, H, part, lanes), bf16), pltpu.SemaphoreType.DMA((count,))],
        ),
        out_shape=jax.ShapeDtypeStruct((H, rows, keys), bf16),
        compiler_params=params(),
        cost_estimate=COST,
        name="lay_bias",
    )(me, *pieces)


def lay_vectors_body(counts, x_ref, out_ref):
    x = x_ref[...]
    D = out_ref.shape[1]
    row = start = 0
    for n in counts:
        per = D // n
        for i in range(x.shape[0] // per):
            pieces = [x[j : j + 1, start : start + n] for j in range(i * per, (i + 1) * per)]
            out_ref[row : row + 1, :] = jnp.concatenate(pieces, axis=1)
            row += 1
        start += n
    out_ref[row:, :] = jnp.zeros((out_ref.shape[0] - row, D), f32)


def lay_vectors(x, *counts):
    D = x.shape[1]

    def body(x_ref, out_ref):
        lay_vectors_body(counts, x_ref, out_ref)

    return pl.pallas_call(
        body,
        out_shape=jax.ShapeDtypeStruct((8, D), f32),
        compiler_params=params(),
        cost_estimate=COST,
        name="lay_vectors",
    )(x)


def norm_back(n, r, g):
    return r * (g - jnp.mean(g, axis=-1, keepdims=True) - n * jnp.mean(g * n, axis=-1, keepdims=True))


def slope(s):
    return s * (1.0 - s)


def mm(a, b, ca, cb, out=f32):
    return lax.dot_general(a, b, ((ca, cb), ((), ())), preferred_element_type=f32).astype(out)


def hop(x, axis, k):
    return lax.ppermute(x, axis, [(i, i ^ k) for i in range(lax.axis_size(axis))])


def at(x, i):
    return lax.dynamic_index_in_dim(x, i, 0, keepdims=False)


def everyone(x, *others):
    steps = [(axis, 1 << i) for axis in ("tok", "samp") for i in range((lax.axis_size(axis) - 1).bit_length())]
    for i, (axis, k) in enumerate(steps):
        x = x + hop(x, axis, k)
        if i == 0:
            x = x + zero(*others).astype(f32)
    return x


def zero(*others):
    corners = [lax.slice(o, (0,) * o.ndim, (1,) * o.ndim).reshape(()).astype(f32) for o in others]
    return sum((jnp.abs(c) > 1e30).astype(jnp.int32) for c in corners)


def gather_tok(x, *others):
    n, t = lax.axis_size("tok"), lax.axis_index("tok")
    up, down = [x], [x]
    for _ in range(1, n):
        up.append(lax.ppermute(up[-1], "tok", [(i, i + 1) for i in range(n - 1)]))
        down.append(lax.ppermute(down[-1], "tok", [(i + 1, i) for i in range(n - 1)]))
    place = t + n + (zero(*others) if others else 0)
    out = jnp.zeros((n,) + x.shape, x.dtype)
    out = lax.dynamic_update_slice_in_dim(out, x[None], place % n, 0)
    for k in range(1, n):
        got = jnp.where(t >= k, up[k], down[n - k])
        out = lax.dynamic_update_slice_in_dim(out, got[None], (place - k) % n, 0)
    return out


def lay_tok(x, *others):
    n, t = lax.axis_size("tok"), lax.axis_index("tok")
    came = [x if k == 0 else hop(x, "tok", k) for k in range(n)]
    out = jnp.zeros((n,) + x.shape, x.dtype)
    place = t + zero(*others)
    for k in range(n):
        out = lax.dynamic_update_slice_in_dim(out, came[k][None], place ^ k, 0)
    return out


def sum_tok(x, *others, dim=0):
    n, t = lax.axis_size("tok"), lax.axis_index("tok")

    def part(i):
        return lax.dynamic_index_in_dim(x, i, dim, keepdims=False)

    came = [hop(part(t ^ k).astype(bf16), "tok", k) for k in range(1, n)]
    total = part(t + (zero(*others) if others else 0)).astype(f32)
    for c in came:
        total = total + c.astype(f32)
    return total


def sum_samp_start(parts, *others):
    n = lax.axis_size("samp")
    if n != 8:
        return jnp.concatenate([p.astype(bf16) for p in parts], axis=-2)
    c = lax.axis_index("samp") % 2

    def half(which):
        picked = [
            lax.dynamic_index_in_dim(p.reshape((n // 2, 2) + p.shape[1:]), which, 1, keepdims=False) for p in parts
        ]
        return jnp.concatenate(picked, axis=-2) if len(picked) > 1 else picked[0]

    other = hop(half(1 - c).astype(bf16), "samp", 1)
    both = half(c + zero(*others)).astype(f32) + other.astype(f32)
    return both.astype(bf16)


def sum_samp_end(both):
    n = lax.axis_size("samp")
    if n != 8:
        return lax.psum_scatter(both, "samp", scatter_dimension=0, tiled=False).astype(f32)
    j = lax.axis_index("samp") // 2
    total = at(both, j).astype(f32)
    for k in range(1, n // 2):
        total = total + hop(at(both, j ^ k), "samp", 2 * k).astype(f32)
    return total


def sum_samp(parts):
    return sum_samp_end(sum_samp_start(parts))


def per_device(
    tokens_in, cotangent, singles, noise_table, noise_level, pad_mask, pairwise, conditioner,
    offsets, shifts, projector, querybias, combiner, expander, reducer, pairhead,
):
    S, R, D = tokens_in.shape
    C = pairwise.shape[2]
    N = pad_mask.shape[1]
    H = pairhead.shape[1]
    CS = conditioner.shape[0]
    T, G = lax.axis_size("tok"), lax.axis_size("samp")
    W = G * T
    t, me = lax.axis_index("tok"), lax.axis_index("samp")
    fold = 4 if G == 8 else 1

    def blocks(w):
        return [w[:, i * D : (i + 1) * D] for i in range(w.shape[1] // D)]

    def rows_of(buf, start, count):
        return buf[:, start : start + count].reshape(W * count, D)

    cond_t = conditioner.T
    cc, pr, rr = cond_t.shape[0], projector.shape[0], reducer.shape[0]
    no, ns = offsets.shape[0], shifts.shape[0]
    vec = jnp.concatenate([offsets, shifts, querybias])
    vec_row = jnp.zeros((8, D), bf16).at[0, : vec.shape[0]].set(vec)
    cond_rows = jnp.concatenate([cond_t[: cc // 2], cond_t[cc // 2 :]], axis=1)
    q_block, k_block, v_block, g_block = blocks(projector)
    mine = lax.dynamic_slice_in_dim(singles[0], me * (R // G), R // G, 0)
    if R % (2 * G) == 0:
        single = jnp.concatenate([mine[: R // G // 2], mine[R // G // 2 :]], axis=1)
    else:
        single = jnp.pad(mine, ((0, 0), (0, D - CS)))
    single_rows = single.shape[0]
    first = jnp.concatenate([q_block, g_block, k_block, v_block, cond_rows, vec_row, single], axis=0)
    second = jnp.concatenate(blocks(expander) + [combiner, reducer], axis=0)
    first_all = lax.all_gather(first, ("samp", "tok"), axis=0)

    pht = pairhead.T
    piece = pair_bias(pairwise[0], pht, fold)
    if fold > 1:
        even = [piece] + [hop(piece, "samp", k) for k in range(2, G, 2)]
        pieces = [p for e in even for p in (e, hop(e, "samp", 1))]
        bias_all = lay_bias(me.astype(jnp.int32)[None], pieces, R)
    else:
        bias_all = jnp.transpose(lax.all_gather(piece, "samp", axis=0), (1, 2, 0, 3)).reshape(H, R, N)
    mask_add = (pad_mask.astype(f32) - 1.0) * 1e9
    every = gather_tok(jnp.concatenate([tokens_in.reshape(S * R, D), second], axis=0), bias_all)
    second_mine = lax.dynamic_slice_in_dim(every, S * R + zero(first_all), second.shape[0], 1)
    second_all = lax.all_gather(second_mine, "samp", axis=0).reshape(W, second.shape[0], D)

    tokens_all = every[:, : S * R].reshape(T, S, R, D).transpose(1, 0, 2, 3).reshape(S * N, D)
    token_norm_all, _ = normal_rows(tokens_all.astype(f32))
    singles_all = first_all[:, -single_rows:].reshape(G, T, single_rows, D).transpose(1, 0, 2, 3)
    if single_rows * 2 == R // G:
        halves = [singles_all[:, :, :, :CS], singles_all[:, :, :, CS:]]
        singles_all = jnp.concatenate(halves, axis=2).reshape(N, CS)
    else:
        singles_all = singles_all[:, :, :, :CS].reshape(N, CS)
    noise_rows = jnp.stack([at(noise_table, noise_level[b]) for b in range(S)])
    cond_all, _ = normal_rows((singles_all.astype(f32)[None] + noise_rows[:, None]).reshape(S * N, CS))
    cond_low_all = cond_all.astype(bf16)
    cond_norm, cond_inv = normal_rows((singles.astype(f32) + noise_rows[:, None]).reshape(S * R, CS))
    cond_low = cond_norm.astype(bf16)
    tokens = tokens_in.reshape(S * R, D).astype(f32)

    def own(x):
        return lax.dynamic_slice_in_dim(x.reshape(S, N, x.shape[-1]), t * R, R, 1).reshape(S * R, x.shape[-1])

    proj_full = jnp.concatenate([rows_of(first_all, i * pr, pr) for i in range(4)], axis=1)
    def cond_rows_of(start, stop):
        a, b = start // cc, -(-stop // cc)
        part = first_all[a:b, 4 * pr : 4 * pr + cc // 2]
        part = jnp.concatenate([part[:, :, :CS], part[:, :, CS:]], axis=1).reshape((b - a) * cc, CS)
        return part[start - a * cc : stop - a * cc]

    cond_pre, cond_rest = cond_rows_of(0, 2 * D), cond_rows_of(2 * D, 6 * D)
    vecs = first_all[:, 4 * pr + cc // 2].astype(f32)
    if fold > 1:
        rows = lay_vectors(vecs, no, ns, pr)
        o, sh, querybias_full = [rows[i : i + 1] for i in range(4)], [rows[4:5], rows[5:6]], rows[6:7]
    else:
        o = jnp.split(vecs[:, :no].reshape(1, W * no), 4, axis=1)
        sh = jnp.split(vecs[:, no : no + ns].reshape(1, W * ns), 2, axis=1)
        querybias_full = vecs[:, no + ns : no + ns + pr].reshape(1, W * pr)

    adapt_pre = mm(cond_low_all, cond_pre, (1,), (1,)) + jnp.concatenate([o[0], sh[0]], axis=1)
    gain_all = jax.nn.sigmoid(adapt_pre[:, :D])
    pre_all = (gain_all * token_norm_all + adapt_pre[:, D:]).astype(bf16)
    pre = own(pre_all)
    kv = mm(pre_all, proj_full[:, 2 * D :], (1,), (0,), bf16).reshape(S, N, 2 * D)
    query = (mm(pre, proj_full[:, :D], (1,), (0,)) + querybias_full).astype(bf16).reshape(S, R, D)
    gating = jax.nn.sigmoid(mm(pre, proj_full[:, D : 2 * D], (1,), (0,)))

    probs, attended = attention(query, kv, bias_all, mask_add)
    attended = attended.reshape(S * R, D)

    adapt_own = mm(cond_low, cond_rest, (1,), (1,)) + jnp.concatenate([o[1], o[2], sh[1], o[3]], axis=1)
    pregate, postscale, postshift, postgate = jnp.split(adapt_own, 4, axis=-1)
    expand_full = jnp.concatenate([rows_of(second_all, i * pr, pr) for i in range(4)], axis=1)
    comb_full = rows_of(second_all, 4 * pr, pr)
    reduce_full = rows_of(second_all, 5 * pr, rr)

    gated = (gating * attended).astype(bf16)
    branch = mm(gated, comb_full, (1,), (0,))
    pregate_sig = jax.nn.sigmoid(pregate)
    residual = tokens + pregate_sig * branch
    post_norm, post_inv = normal_rows(residual)
    post_gain = jax.nn.sigmoid(postscale)
    posthidden = (post_gain * post_norm + postshift).astype(bf16)
    upgate = mm(posthidden, expand_full, (1,), (0,))
    FF = upgate.shape[-1] // 2
    preact, upper = upgate[:, :FF], upgate[:, FF:]
    preact_sig = jax.nn.sigmoid(preact)
    swished = preact * preact_sig
    activated = (swished * upper).astype(bf16)
    trans = mm(activated, reduce_full, (1,), (0,))
    postgate_sig = jax.nn.sigmoid(postgate)
    mixed = (residual + postgate_sig * trans).astype(bf16)

    def owned(grad):
        return [g.reshape(G, T, g.shape[0] // W, D) for g in blocks(grad)]

    g_out = cotangent.reshape(S * R, D)
    trans_back = (postgate_sig * g_out).astype(bf16)
    postgate_back = g_out * trans * slope(postgate_sig)
    reducer_part = mm(activated, trans_back, (0,), (0,), bf16)
    act_back = mm(trans_back, reduce_full, (1,), (1,))
    up_back = jnp.concatenate(
        [act_back * upper * preact_sig * (1.0 + preact * (1.0 - preact_sig)), act_back * swished], axis=-1
    ).astype(bf16)
    expander_part = mm(posthidden, up_back, (0,), (0,), bf16)
    posthidden_back = mm(up_back, expand_full, (1,), (1,))
    postscale_back = posthidden_back * post_norm * slope(post_gain)
    residual_back = g_out + norm_back(post_norm, post_inv, posthidden_back * post_gain)
    branch_back = (pregate_sig * residual_back).astype(bf16)
    pregate_back = residual_back * branch * slope(pregate_sig)
    combiner_part = mm(gated, branch_back, (0,), (0,), bf16)
    second_part = jnp.concatenate(owned(expander_part) + owned(combiner_part) + owned(reducer_part), axis=2)
    second_owned = second_part.reshape(G, -1, D)
    second_part = lax.psum_scatter(second_owned, "samp", scatter_dimension=0, tiled=False)

    gated_back = mm(branch_back, comb_full, (1,), (1,))
    attended_back = (gating * gated_back).astype(bf16)
    gating_low = (attended * gated_back * slope(gating)).astype(bf16)
    query_back, dkv, *bias_back = attention_back(
        me.astype(jnp.int32)[None], probs, attended_back.reshape(S, R, D), kv, query, second_owned, fold, G
    )
    query_back = query_back.reshape(S * R, D)
    dkv = dkv.reshape(S, 2 * D, N)

    later = jnp.concatenate([pregate_back, postscale_back, posthidden_back, postgate_back], axis=-1)
    later_sums = jnp.split(jnp.sum(later, axis=0), 4)
    later_low = later.astype(bf16)
    later_part = mm(later_low, cond_low, (0,), (0,), bf16)
    later_back = mm(later_low, cond_rest, (1,), (0,))

    pre_back_all = mm(dkv, proj_full[:, 2 * D :], (1,), (1,), bf16)
    if fold > 1:
        kept, given = bias_back
        bias_both = (kept.astype(f32) + hop(given, "samp", 1).astype(f32) + zero(pre_back_all).astype(f32)).astype(bf16)
        bias_sum = sum_samp_end(bias_both)
    else:
        bias_sum = sum_samp([bias_back[0].reshape(H * R, G, C).transpose(1, 0, 2)]).reshape(H, R, C)
    qg_low = jnp.concatenate([query_back.astype(bf16), gating_low], axis=-1)
    pair_grad, pairhead_part = pair_back(pairwise[0], bias_sum.transpose(1, 0, 2), pht, fold)
    qg_part = mm(pre, qg_low, (0,), (0,), bf16)
    kv_part = mm(pre_all.reshape(S, N, D), dkv, (0, 1), (0, 2), bf16)
    proj_owned = jnp.concatenate(owned(qg_part) + owned(kv_part), axis=2).reshape(G, -1, D)
    proj_part = lax.psum_scatter(proj_owned, "samp", scatter_dimension=0, tiled=False)
    pre_back = sum_tok(pre_back_all.reshape(S, T, R, D), pairhead_part, proj_owned, dim=1).reshape(S * R, D)
    pre_back = pre_back + mm(qg_low, proj_full[:, : 2 * D], (1,), (1,))

    token_norm, token_inv = normal_rows(tokens)
    gain = own(gain_all)
    prescale_back = pre_back * token_norm * slope(gain)
    tokens_grad = residual_back + norm_back(token_norm, token_inv, pre_back * gain)
    early = jnp.concatenate([prescale_back, pre_back], axis=-1)
    early_sums = jnp.split(jnp.sum(early, axis=0), 2)
    early_low = early.astype(bf16)
    early_part = mm(early_low, cond_low, (0,), (0,), bf16)
    cond_grad = norm_back(cond_norm, cond_inv, later_back + mm(early_low, cond_pre, (1,), (0,)))

    offsets_part = jnp.concatenate([early_sums[0], later_sums[0], later_sums[1], later_sums[3]])
    shifts_part = jnp.concatenate([early_sums[1], later_sums[2]])
    querybias_part = jnp.sum(query_back, axis=0)
    cond_part = jnp.concatenate([early_part, later_part], axis=0).reshape(G, T, cc, CS)
    cond_part = jnp.concatenate([cond_part[:, :, : cc // 2], cond_part[:, :, cc // 2 :]], axis=-1)
    vec_part = jnp.concatenate(
        [offsets_part.reshape(G, T, no), shifts_part.reshape(G, T, ns), querybias_part.reshape(G, T, pr)], axis=-1
    )
    vec_part = jnp.zeros((G, T, 8, D), bf16).at[:, :, 0, : vec.shape[0]].set(vec_part.astype(bf16))
    cond_part = jnp.concatenate([cond_part, vec_part], axis=2).reshape(G, -1, D)
    cond_grad = cond_grad.reshape(S, R, CS)
    singles_part = jnp.sum(cond_grad, axis=0)
    cs = CS // G
    extra = jnp.pad(singles_part.T, ((0, 0), (0, D - R))).reshape(G, cs, D).astype(bf16)
    cond_both = sum_samp_start([cond_part, extra])
    second_part, proj_part = second_part.reshape(T, -1, D), proj_part.reshape(T, -1, D)
    both_part = jnp.concatenate([second_part + zero(cond_part).astype(bf16), proj_part], axis=1)
    both_sum = lax.psum_scatter(both_part, "tok", scatter_dimension=0, tiled=False).astype(f32)
    second_sum, proj_sum = both_sum[: second.shape[0]], both_sum[second.shape[0] :]
    both = sum_samp_end(cond_both)
    cond_sum, singles_t = both[: cond_part.shape[1]], both[cond_part.shape[1] :, :R]
    cond_half = cond_sum
    cond_sum = sum_tok(cond_sum.reshape(T, -1, D))

    by_sample = jnp.concatenate(
        [jnp.sum(cond_grad, axis=1), jnp.broadcast_to(jnp.where(t == 0, noise_level, 0)[:, None], (S, 128)).astype(f32)],
        axis=1,
    )
    placed = lax.dynamic_update_slice_in_dim(jnp.zeros((G * S, CS + 128), f32), by_sample, me * S, 0)
    small = everyone(jnp.concatenate([placed, jnp.pad(pairhead_part, ((0, 0), (0, CS)))], axis=0), cond_half)
    level_all = small[: G * S, CS].astype(jnp.int32)
    levels = jnp.arange(noise_table.shape[0], dtype=jnp.int32)
    level_hot = (levels[:, None] == level_all[None, :]).astype(f32)
    noise_grad = jnp.dot(level_hot, small[: G * S, :CS], precision=lax.Precision.HIGHEST)
    pairhead_grad = small[G * S :, : pairhead_part.shape[1]].T

    def unblocks(x, order):
        return jnp.concatenate([x[i * pr : (i + 1) * pr] for i in order], axis=1)

    cond_out = cond_sum[: cc // 2]
    vec_out = cond_sum[cc // 2]
    return (
        mixed.reshape(S, R, D),
        tokens_grad.reshape(S, R, D),
        singles_t.T[None],
        pair_grad[None],
        noise_grad,
        jnp.concatenate([cond_out[:, :CS], cond_out[:, CS:]], axis=0).T,
        vec_out[:no],
        vec_out[no : no + ns],
        unblocks(proj_sum, (0, 2, 3, 1)),
        vec_out[no + ns : no + ns + pr],
        second_sum[4 * pr : 5 * pr],
        unblocks(second_sum, (0, 1, 2, 3)),
        second_sum[5 * pr :],
        pairhead_grad,
    )


def solution(mesh):
    shard = ("samp", "tok")
    in_specs = (
        P("samp", "tok", None), P("samp", "tok", None), P(None, "tok", None), P(), P("samp"), P(),
        P(None, "tok", "samp", None), P(None, shard), P(shard), P(shard), P(shard, None), P(shard),
        P(shard, None), P(shard, None), P(shard, None), P(),
    )
    out_specs = (
        P("samp", "tok", None), P("samp", "tok", None), P(None, "tok", "samp"), P(None, "tok", "samp", None), P(),
        P(None, shard), P(shard), P(shard), P(shard, None), P(shard), P(shard, None), P(shard, None),
        P(shard, None), P(),
    )
    return jax.shard_map(per_device, mesh=mesh, in_specs=in_specs, out_specs=out_specs, check_vma=False)
```

```python
from jax.experimental.layout import Layout, with_layout_constraint
import jax
import jax.numpy as jnp
from jax import lax
from jax.experimental import pallas as pl
from jax.experimental.pallas import tpu as pltpu
from jax.sharding import PartitionSpec as P

DH = 48
EPS = 1e-5
WIN = 256
ROWS = 32
VMEM_BYTES = 56 * 1024 * 1024
f32 = jnp.float32
bf16 = jnp.bfloat16
COST = pl.CostEstimate(flops=1024, bytes_accessed=1024, transcendentals=0)
NT = (((1,), (1,)), ((), ()))
TN = (((0,), (0,)), ((), ()))


def params():
    return pltpu.CompilerParams(vmem_limit_bytes=VMEM_BYTES)


def window(h, width):
    w = pl.multiple_of(jnp.minimum((h * DH) // 128 * 128, width - WIN), 128)
    lane = lax.broadcasted_iota(jnp.int32, (1, WIN), 1) + w
    return w, (lane >= h * DH) & (lane < h * DH + DH)


def attention_body(q_ref, k_ref, v_ref, bias_ref, mask_ref, p_ref, att_ref, scores):
    samples, rows, width = q_ref.shape
    heads = bias_ref.shape[0]
    mask = mask_ref[...]
    windows = [window(pl.program_id(0) * heads + u, width) for u in range(heads)]
    for u, (w, inside) in enumerate(windows):
        for b in range(samples):
            q = jnp.where(inside, q_ref[b, :, pl.ds(w, WIN)], 0)
            scores[u * samples + b] = lax.dot_general(q, k_ref[b, :, pl.ds(w, WIN)], NT, preferred_element_type=f32)
    for u in range(heads):
        for i in range(0, rows, ROWS):
            bias = bias_ref[u, i : i + ROWS].astype(f32) + mask
            for b in range(samples):
                s = scores[u * samples + b, i : i + ROWS] * (DH ** -0.5) + bias
                e = jnp.exp(s - jnp.max(s, axis=1, keepdims=True))
                p_ref[u, b, i : i + ROWS] = (e * (1.0 / jnp.sum(e, axis=1, keepdims=True))).astype(bf16)
    for u, (w, inside) in enumerate(windows):
        for b in range(samples):
            o = jnp.dot(p_ref[u, b], v_ref[b, :, pl.ds(w, WIN)], preferred_element_type=f32)
            att_ref[b, :, pl.ds(w, WIN)] = jnp.where(inside, o, att_ref[b, :, pl.ds(w, WIN)])


def attention(q, kv, bias, mask):
    S, R, D = q.shape
    N, H = kv.shape[1], bias.shape[0]
    heads = 4

    def whole(*shape):
        return pl.BlockSpec(shape, lambda h: (0,) * len(shape))

    return pl.pallas_call(
        attention_body,
        grid=(H // heads,),
        in_specs=[
            whole(S, R, D),
            whole(S, N, D),
            pl.BlockSpec((S, N, D), lambda h: (0, 0, 1)),
            pl.BlockSpec((heads, R, N), lambda h: (h, 0, 0)),
            whole(1, N),
        ],
        out_specs=[pl.BlockSpec((heads, S, R, N), lambda h: (h, 0, 0, 0)), whole(S, R, D)],
        out_shape=[jax.ShapeDtypeStruct((H, S, R, N), bf16), jax.ShapeDtypeStruct((S, R, D), f32)],
        scratch_shapes=[pltpu.VMEM((heads * S, R, N), f32)],
        compiler_params=params(),
        cost_estimate=COST,
        name="attention",
    )(q, kv, kv, bias, mask)


def attention_back_body(fold, me_ref, p_ref, do_ref, k_ref, v_ref, q_ref, dq_ref, dkv_ref, *rest):
    *bb_refs, qt, dot_, dp_all, low_all, acc = rest
    samples, rows, width = do_ref.shape
    heads = p_ref.shape[0]
    step = pl.program_id(0)

    @pl.when(step == 0)
    def _():
        for b in range(samples):
            qt[b] = q_ref[b].astype(f32).T.astype(bf16)
            dot_[b] = do_ref[b].astype(f32).T.astype(bf16)

    windows = [window(step * heads + u, width) for u in range(heads)]
    for u, (w, inside) in enumerate(windows):
        for b in range(samples):
            do = jnp.where(inside, do_ref[b, :, pl.ds(w, WIN)], 0)
            dp_all[u * samples + b] = lax.dot_general(do, v_ref[b, :, pl.ds(w, WIN)], NT, preferred_element_type=f32)
    for u in range(heads):
        for i in range(0, rows, ROWS):
            total = None
            for b in range(samples):
                dp = dp_all[u * samples + b, i : i + ROWS]
                p = p_ref[u, b, i : i + ROWS].astype(f32)
                ds = p * (dp - jnp.sum(p * dp, axis=1, keepdims=True))
                low_all[u * samples + b, i : i + ROWS] = ds.astype(bf16)
                total = ds if total is None else total + ds
            acc[u, i : i + ROWS] = total
    for u, (w, inside) in enumerate(windows):
        own = pl.ds(pl.multiple_of((step * heads + u) * DH, 16), DH)
        for b in range(samples):
            low = low_all[u * samples + b]
            dq = jnp.dot(low, k_ref[b, :, pl.ds(w, WIN)], preferred_element_type=f32) * (DH ** -0.5)
            dq_ref[b, :, pl.ds(w, WIN)] = jnp.where(inside, dq, dq_ref[b, :, pl.ds(w, WIN)])
            dk = jnp.dot(qt[b, own, :], low, preferred_element_type=f32) * (DH ** -0.5)
            dv = jnp.dot(dot_[b, own, :], p_ref[u, b], preferred_element_type=f32)
            dkv_ref[b, 0, u * DH : (u + 1) * DH] = dk.astype(bf16)
            dkv_ref[b, 1, u * DH : (u + 1) * DH] = dv.astype(bf16)
        if fold == 1:
            bb_refs[0][u] = acc[u].astype(bf16)
            continue
        kept_ref, given_ref = bb_refs
        count, _, part, lanes = kept_ref.shape
        c = lanes // fold
        odd = me_ref[0] % 2 == 1

        def piece(s):
            return jnp.concatenate(
                [acc[u, i * part : (i + 1) * part, s * c : (s + 1) * c] for i in range(fold)], axis=1
            )

        for j in range(count):
            first, second = piece(2 * j), piece(2 * j + 1)
            kept_ref[j, u] = jnp.where(odd, second, first).astype(bf16)
            given_ref[j, u] = jnp.where(odd, first, second).astype(bf16)


def attention_back(me, p, do, kv, q, first, fold, groups):
    H, S, R, N = p.shape
    D = do.shape[2]
    heads = 2

    def whole(*shape):
        return pl.BlockSpec(shape, lambda h, m: (0,) * len(shape))

    if fold == 1:
        bb_specs, bb_shapes = [pl.BlockSpec((heads, R, N), lambda h, m: (h, 0, 0))], [(H, R, N)]
    else:
        tail = (R // fold, fold * (N // groups))
        bb_specs = [pl.BlockSpec((groups // 2, heads) + tail, lambda h, m: (0, h, 0, 0))] * 2
        bb_shapes = [(groups // 2, H) + tail] * 2

    def body(me_ref, p_ref, do_ref, k_ref, v_ref, q_ref, _, *refs):
        attention_back_body(fold, me_ref, p_ref, do_ref, k_ref, v_ref, q_ref, *refs)

    return pl.pallas_call(
        body,
        grid_spec=pltpu.PrefetchScalarGridSpec(
            num_scalar_prefetch=1,
            grid=(H // heads,),
            in_specs=[
                pl.BlockSpec((heads, S, R, N), lambda h, m: (h, 0, 0, 0)),
                whole(S, R, D),
                whole(S, N, D),
                pl.BlockSpec((S, N, D), lambda h, m: (0, 0, 1)),
                whole(S, R, D),
                pl.BlockSpec(memory_space=pl.ANY),
            ],
            out_specs=[whole(S, R, D), pl.BlockSpec((S, 2, heads * DH, N), lambda h, m: (0, 0, h, 0))] + bb_specs,
            scratch_shapes=[
                pltpu.VMEM((S, D, R), bf16),
                pltpu.VMEM((S, D, R), bf16),
                pltpu.VMEM((heads * S, R, N), f32),
                pltpu.VMEM((heads * S, R, N), bf16),
                pltpu.VMEM((heads, R, N), f32),
            ],
        ),
        out_shape=[
            jax.ShapeDtypeStruct((S, R, D), f32),
            jax.ShapeDtypeStruct((S, 2, D, N), bf16),
        ]
        + [jax.ShapeDtypeStruct(shape, bf16) for shape in bb_shapes],
        compiler_params=params(),
        cost_estimate=COST,
        name="attention_back",
    )(me, p, do, kv, kv, q, first)


def normal_rows(x):
    c = x - jnp.mean(x, axis=-1, keepdims=True)
    r = lax.rsqrt(jnp.mean(c * c, axis=-1, keepdims=True) + EPS)
    return c * r, r


def split(x):
    hi = x.astype(bf16)
    return hi, (x - hi.astype(f32)).astype(bf16)


def lane_mean(x):
    ones = jnp.full((x.shape[1], x.shape[1]), 1.0, bf16)
    hi, lo = split(x)
    total = jnp.dot(hi, ones, preferred_element_type=f32) + jnp.dot(lo, ones, preferred_element_type=f32)
    return total * (1.0 / x.shape[1])


def pair_bias_body(x_ref, ph_ref, out_ref, buf):
    fold, n, C, E = x_ref.shape
    ph = ph_ref[...]
    for i in range(n):
        x = x_ref[:, i].reshape(fold * C, E) if fold > 1 else x_ref[0, i]
        nrm, _ = normal_rows(x.astype(f32))
        buf[:, i, :] = lax.dot_general(ph, nrm.astype(bf16), NT, preferred_element_type=f32)
    out_ref[...] = buf[...].astype(bf16)


def pair_bias(x, pht, fold):
    R, C, E = x.shape
    H = pht.shape[0]
    rows = R // fold
    blk = 16
    return pl.pallas_call(
        pair_bias_body,
        grid=(rows // blk,),
        in_specs=[
            pl.BlockSpec((fold, blk, C, E), lambda i: (0, i, 0, 0)), pl.BlockSpec((H, E), lambda i: (0, 0)),
        ],
        out_specs=pl.BlockSpec((H, blk, fold * C), lambda i: (0, i, 0)),
        out_shape=jax.ShapeDtypeStruct((H, rows, fold * C), bf16),
        scratch_shapes=[pltpu.VMEM((H, blk, fold * C), f32)],
        compiler_params=params(),
        cost_estimate=COST,
        name="pair_bias",
    )(x.reshape(fold, rows, C, E), pht)


def pair_back_body(x_ref, bb_ref, ph_ref, _, out_ref, dph_ref):
    fold, n, C, E = x_ref.shape
    H = ph_ref.shape[0]
    ph = ph_ref[...].astype(f32)
    ph_hi, ph_lo = split(ph - jnp.mean(ph, axis=-1, keepdims=True))
    ph4 = jnp.concatenate([ph_hi, ph_lo, ph_hi, ph_lo], axis=0)
    acc = jnp.zeros((2 * H, E), f32)
    for i in range(n):
        x = x_ref[:, i].reshape(fold * C, E) if fold > 1 else x_ref[0, i]
        nrm, r = normal_rows(x.astype(f32))
        hi, lo = split(bb_ref[i])
        g = lax.dot_general(
            jnp.concatenate([hi, hi, lo, lo], axis=0), ph4, TN, preferred_element_type=f32
        )
        grad = r * (g - nrm * lane_mean(g * nrm))
        if fold > 1:
            out_ref[:, i] = grad.reshape(fold, C, E)
        else:
            out_ref[0, i] = grad
        acc += jnp.dot(jnp.concatenate([hi, lo], axis=0), nrm.astype(bf16), preferred_element_type=f32)
    part = acc[:H] + acc[H:]

    @pl.when(pl.program_id(0) == 0)
    def _():
        dph_ref[...] = part

    @pl.when(pl.program_id(0) != 0)
    def _():
        dph_ref[...] += part


def pair_back(x, bb, pht, first, fold):
    R, C, E = x.shape
    H = pht.shape[0]
    rows = R // fold
    blk = 8
    grad, dph = pl.pallas_call(
        pair_back_body,
        grid=(rows // blk,),
        in_specs=[
            pl.BlockSpec((fold, blk, C, E), lambda i: (0, i, 0, 0)),
            pl.BlockSpec((blk, H, fold * C), lambda i: (i, 0, 0)),
            pl.BlockSpec((H, E), lambda i: (0, 0)),
            pl.BlockSpec(memory_space=pl.ANY),
        ],
        out_specs=[pl.BlockSpec((fold, blk, C, E), lambda i: (0, i, 0, 0)), pl.BlockSpec((H, E), lambda i: (0, 0))],
        out_shape=[jax.ShapeDtypeStruct((fold, rows, C, E), f32), jax.ShapeDtypeStruct((H, E), f32)],
        compiler_params=params(),
        cost_estimate=COST,
        name="pair_back",
    )(x.reshape(fold, rows, C, E), bb, pht, first)
    return grad.reshape(R, C, E), dph


def lay_bias_body(me_ref, *refs):
    pieces, (out_ref, slots, sems) = refs[:-3], refs[-3:]
    h = pl.program_id(0)
    part, lanes = slots.shape[2:]
    fold = out_ref.shape[1] // part
    c = lanes // fold

    @pl.when(h == 0)
    def _():
        copies = [
            pltpu.make_async_copy(p, slots.at[jnp.bitwise_xor(me_ref[0], k)], sems.at[k]) for k, p in enumerate(pieces)
        ]
        for copy in copies:
            copy.start()
        for copy in copies:
            copy.wait()

    laid = [slots[s, h].astype(f32) for s in range(len(pieces))]
    for i in range(fold):
        out_ref[0, i * part : (i + 1) * part, :] = jnp.concatenate(
            [p[:, i * c : (i + 1) * c] for p in laid], axis=1
        ).astype(bf16)


def lay_bias(me, pieces, rows):
    H, part, lanes = pieces[0].shape
    count = len(pieces)
    keys = count * lanes // (rows // part)
    return pl.pallas_call(
        lay_bias_body,
        grid_spec=pltpu.PrefetchScalarGridSpec(
            num_scalar_prefetch=1,
            grid=(H,),
            in_specs=[pl.BlockSpec(memory_space=pl.ANY)] * count,
            out_specs=pl.BlockSpec((1, rows, keys), lambda h, s: (h, 0, 0)),
            scratch_shapes=[pltpu.VMEM((count, H, part, lanes), bf16), pltpu.SemaphoreType.DMA((count,))],
        ),
        out_shape=jax.ShapeDtypeStruct((H, rows, keys), bf16),
        compiler_params=params(),
        cost_estimate=COST,
        name="lay_bias",
    )(me, *pieces)


def lay_vectors_body(counts, x_ref, out_ref):
    x = x_ref[...]
    D = out_ref.shape[1]
    row = start = 0
    for n in counts:
        per = D // n
        for i in range(x.shape[0] // per):
            pieces = [x[j : j + 1, start : start + n] for j in range(i * per, (i + 1) * per)]
            out_ref[row : row + 1, :] = jnp.concatenate(pieces, axis=1)
            row += 1
        start += n
    out_ref[row:, :] = jnp.zeros((out_ref.shape[0] - row, D), f32)


def lay_vectors(x, *counts):
    D = x.shape[1]

    def body(x_ref, out_ref):
        lay_vectors_body(counts, x_ref, out_ref)

    return pl.pallas_call(
        body,
        out_shape=jax.ShapeDtypeStruct((8, D), f32),
        compiler_params=params(),
        cost_estimate=COST,
        name="lay_vectors",
    )(x)


def center(n, r, g):
    return r * (g - jnp.mean(g, axis=-1, keepdims=True) - n * jnp.mean(g * n, axis=-1, keepdims=True))


def finish(parts, tokens, gain, residual_back, later_back, cond, cond_low, cond_pre, first, samples):
    rows, D = tokens.shape
    CS = cond.shape[1]
    count = len(parts)

    def body(*refs):
        x = refs[0][...].astype(f32)
        for p in refs[1:count]:
            x = x + p[...].astype(f32)
        tok, gain_ref, resid, later, cond_ref, low_ref, pre_ref = refs[count : count + 7]
        grad, sums, part, single, by_sample = refs[count + 7 + len(first) :]
        n, r = normal_rows(tok[...].astype(f32))
        g = gain_ref[...]
        scale = x * n * (g * (1.0 - g))
        grad[...] = resid[...] + center(n, r, x * g)
        sums[...] = jnp.zeros_like(sums)
        sums[0:1, :] = jnp.sum(scale, axis=0, keepdims=True)
        sums[1:2, :] = jnp.sum(x, axis=0, keepdims=True)
        early = jnp.concatenate([scale.astype(bf16), x.astype(bf16)], axis=1)
        part[...] = lax.dot_general(early, low_ref[...], TN, preferred_element_type=f32).astype(bf16)
        back = later[...] + jnp.dot(early, pre_ref[...], preferred_element_type=f32)
        cond_grad = center(*normal_rows(cond_ref[...]), back)
        each = rows // samples
        total = cond_grad[:each]
        for b in range(1, samples):
            total = total + cond_grad[b * each : (b + 1) * each]
        single[...] = jnp.concatenate([total.T, jnp.zeros((CS, CS - each), f32)], axis=1).astype(bf16)
        by_sample[...] = jnp.zeros_like(by_sample)
        for b in range(samples):
            by_sample[b : b + 1, :] = jnp.sum(cond_grad[b * each : (b + 1) * each], axis=0, keepdims=True)

    shapes = [(rows, D), (8, D), (2 * D, CS), (CS, CS), (8, CS)]
    kinds = [f32, f32, bf16, bf16, f32]
    vmem = pl.BlockSpec(memory_space=pltpu.VMEM)
    return pl.pallas_call(
        body,
        in_specs=[vmem] * (count + 7) + [pl.BlockSpec(memory_space=pl.ANY)] * len(first),
        out_specs=[vmem] * 5,
        out_shape=[jax.ShapeDtypeStruct(s, kind) for s, kind in zip(shapes, kinds)],
        compiler_params=params(),
        cost_estimate=COST,
        name="finish",
    )(*parts, tokens, gain, residual_back, later_back, cond, cond_low, cond_pre, *first)


def pinned(x):
    return with_layout_constraint(x, Layout(major_to_minor=tuple(range(x.ndim))))


def norm_back(n, r, g):
    return r * (g - jnp.mean(g, axis=-1, keepdims=True) - n * jnp.mean(g * n, axis=-1, keepdims=True))


def slope(s):
    return s * (1.0 - s)


def mm(a, b, ca, cb, out=f32):
    return lax.dot_general(a, b, ((ca, cb), ((), ())), preferred_element_type=f32).astype(out)


def hop(x, axis, k):
    return lax.ppermute(x, axis, [(i, i ^ k) for i in range(lax.axis_size(axis))])


def at(x, i):
    return lax.dynamic_index_in_dim(x, i, 0, keepdims=False)


def everyone(x, *others):
    steps = [(axis, 1 << i) for axis in ("tok", "samp") for i in range((lax.axis_size(axis) - 1).bit_length())]
    for i, (axis, k) in enumerate(steps):
        x = x + hop(x, axis, k)
        if i == 0:
            x = x + zero(*others).astype(f32)
    return x


def zero(*others):
    corners = [lax.slice(o, (0,) * o.ndim, (1,) * o.ndim).reshape(()).astype(f32) for o in others]
    return sum((jnp.abs(c) > 1e30).astype(jnp.int32) for c in corners)


def gather_tok(parts, others):
    n, t = lax.axis_size("tok"), lax.axis_index("tok")
    width = parts[0][0].shape[-1]
    rows = [p.size // width for p, _ in parts]
    x = jnp.concatenate([p.reshape(-1, width) for p, _ in parts], axis=0)
    up, down = [x], [x]
    for _ in range(1, n):
        up.append(lax.ppermute(up[-1], "tok", [(i, i + 1) for i in range(n - 1)]))
        down.append(lax.ppermute(down[-1], "tok", [(i + 1, i) for i in range(n - 1)]))
    outs, start = [], 0
    for i, ((p, dim), count) in enumerate(zip(parts, rows)):
        place = t + n + zero(*others[i])
        out = jnp.zeros(p.shape[:dim] + (n,) + p.shape[dim:], p.dtype)
        for k in range(n):
            got = [u[start : start + count].reshape(p.shape) for u in (up[k], down[n - k if k else 0])]
            got = got[0] if k == 0 else jnp.where(t >= k, *got)
            out = lax.dynamic_update_slice_in_dim(out, jnp.expand_dims(got, dim), (place - k) % n, dim)
        outs.append(out)
        start += count
    return outs


def sum_tok(x, *others, dim=0, apart=False):
    n, t = lax.axis_size("tok"), lax.axis_index("tok")
    x = x.reshape(x.shape[:dim] + (n // 2, 2) + x.shape[dim + 1 :])

    def part(v, i, d):
        return lax.dynamic_index_in_dim(v, i, d, keepdims=False)

    came = hop(part(x, 1 - t % 2, dim + 1), "tok", 1)
    pair = part(x, t % 2, dim + 1).astype(f32) + came.astype(f32)
    given = [hop(part(pair, (t // 2) ^ k, dim).astype(bf16), "tok", 2 * k) for k in range(1, n // 2)]
    total = part(pair, t // 2 + (zero(*others) if others else 0), dim)
    if apart:
        return [total] + given
    for g in given:
        total = total + g.astype(f32)
    return total


def sum_samp_start(parts, *others):
    n = lax.axis_size("samp")
    if n != 8:
        return jnp.concatenate([p.astype(bf16) for p in parts], axis=-2)
    c = lax.axis_index("samp") % 2

    def half(which):
        picked = [
            lax.dynamic_index_in_dim(p.reshape((n // 2, 2) + p.shape[1:]), which, 1, keepdims=False) for p in parts
        ]
        return jnp.concatenate(picked, axis=-2) if len(picked) > 1 else picked[0]

    other = hop(half(1 - c).astype(bf16), "samp", 1)
    both = half(c + zero(*others)).astype(f32) + other.astype(f32)
    return pinned(both.astype(bf16))


def sum_samp_end(both):
    n = lax.axis_size("samp")
    if n != 8:
        return lax.psum_scatter(both, "samp", scatter_dimension=0, tiled=False).astype(f32)
    j = lax.axis_index("samp") // 2
    total = at(both, j).astype(f32)
    for k in range(1, n // 2):
        total = total + hop(at(both, j ^ k), "samp", 2 * k).astype(f32)
    return total


def sum_samp(parts):
    return sum_samp_end(sum_samp_start(parts))


def per_device(
    tokens_in, cotangent, singles, noise_table, noise_level, pad_mask, pairwise, conditioner,
    offsets, shifts, projector, querybias, combiner, expander, reducer, pairhead,
):
    S, R, D = tokens_in.shape
    C = pairwise.shape[2]
    N = pad_mask.shape[1]
    H = pairhead.shape[1]
    CS = conditioner.shape[0]
    T, G = lax.axis_size("tok"), lax.axis_size("samp")
    W = G * T
    t, me = lax.axis_index("tok"), lax.axis_index("samp")
    fold = 4 if G == 8 else 1

    def blocks(w):
        return [w[:, i * D : (i + 1) * D] for i in range(w.shape[1] // D)]

    def rows_of(buf, start, count):
        return buf[:, start : start + count].reshape(W * count, D)

    cond_t = conditioner.T
    cc, pr, rr = cond_t.shape[0], projector.shape[0], reducer.shape[0]
    no, ns = offsets.shape[0], shifts.shape[0]
    vec = jnp.concatenate([offsets, shifts, querybias])
    vec_row = jnp.zeros((8, D), bf16).at[0, : vec.shape[0]].set(vec)
    cond_rows = jnp.concatenate([cond_t[: cc // 2], cond_t[cc // 2 :]], axis=1)
    q_block, k_block, v_block, g_block = blocks(projector)
    mine = lax.dynamic_slice_in_dim(singles[0], me * (R // G), R // G, 0)
    if R % (2 * G) == 0:
        single = jnp.concatenate([mine[: R // G // 2], mine[R // G // 2 :]], axis=1)
    else:
        single = jnp.pad(mine, ((0, 0), (0, D - CS)))
    single_rows = single.shape[0]
    first = jnp.concatenate([q_block, g_block, k_block, v_block, cond_rows, vec_row, single], axis=0)
    second = jnp.concatenate(blocks(expander) + [combiner, reducer], axis=0)
    first_all = lax.all_gather(first, ("samp", "tok"), axis=0)

    pht = pairhead.T
    piece = pair_bias(pairwise[0], pht, fold)
    if fold > 1:
        even = [piece] + [hop(piece, "samp", k) for k in range(2, G, 2)]
        pieces = [p for e in even for p in (e, hop(e, "samp", 1))]
        bias_all = lay_bias(me.astype(jnp.int32)[None], pieces, R)
    else:
        bias_all = jnp.transpose(lax.all_gather(piece, "samp", axis=0), (1, 2, 0, 3)).reshape(H, R, N)
    mask_add = (pad_mask.astype(f32) - 1.0) * 1e9
    ready = lax.dynamic_index_in_dim(first_all, zero(bias_all), 0)
    tokens_all, second_mine = gather_tok([(tokens_in, 1), (second, 0)], [[bias_all], [ready]])
    second_all = lax.all_gather(second_mine, "samp", axis=0).reshape(W, second.shape[0], D)

    tokens_all = tokens_all.reshape(S * N, D)
    token_norm_all, _ = normal_rows(tokens_all.astype(f32))
    singles_all = first_all[:, -single_rows:].reshape(G, T, single_rows, D).transpose(1, 0, 2, 3)
    if single_rows * 2 == R // G:
        halves = [singles_all[:, :, :, :CS], singles_all[:, :, :, CS:]]
        singles_all = jnp.concatenate(halves, axis=2).reshape(N, CS)
    else:
        singles_all = singles_all[:, :, :, :CS].reshape(N, CS)
    noise_rows = jnp.stack([at(noise_table, noise_level[b]) for b in range(S)])
    cond_all, _ = normal_rows((singles_all.astype(f32)[None] + noise_rows[:, None]).reshape(S * N, CS))
    cond_low_all = cond_all.astype(bf16)
    cond = (singles.astype(f32) + noise_rows[:, None]).reshape(S * R, CS)
    cond_low = normal_rows(cond)[0].astype(bf16)
    tokens = tokens_in.reshape(S * R, D).astype(f32)

    def own(x):
        return lax.dynamic_slice_in_dim(x.reshape(S, N, x.shape[-1]), t * R, R, 1).reshape(S * R, x.shape[-1])

    proj_full = jnp.concatenate([rows_of(first_all, i * pr, pr) for i in range(4)], axis=1)
    def cond_rows_of(start, stop):
        a, b = start // cc, -(-stop // cc)
        part = first_all[a:b, 4 * pr : 4 * pr + cc // 2]
        part = jnp.concatenate([part[:, :, :CS], part[:, :, CS:]], axis=1).reshape((b - a) * cc, CS)
        return part[start - a * cc : stop - a * cc]

    cond_pre, cond_rest = cond_rows_of(0, 2 * D), cond_rows_of(2 * D, 6 * D)
    vecs = first_all[:, 4 * pr + cc // 2].astype(f32)
    if fold > 1:
        rows = lay_vectors(vecs, no, ns, pr)
        o, sh, querybias_full = [rows[i : i + 1] for i in range(4)], [rows[4:5], rows[5:6]], rows[6:7]
    else:
        o = jnp.split(vecs[:, :no].reshape(1, W * no), 4, axis=1)
        sh = jnp.split(vecs[:, no : no + ns].reshape(1, W * ns), 2, axis=1)
        querybias_full = vecs[:, no + ns : no + ns + pr].reshape(1, W * pr)

    adapt_pre = mm(cond_low_all, cond_pre, (1,), (1,)) + jnp.concatenate([o[0], sh[0]], axis=1)
    gain_all = jax.nn.sigmoid(adapt_pre[:, :D])
    pre_all = (gain_all * token_norm_all + adapt_pre[:, D:]).astype(bf16)
    pre = own(pre_all)
    kv = mm(pre_all, proj_full[:, 2 * D :], (1,), (0,), bf16).reshape(S, N, 2 * D)
    query = (mm(pre, proj_full[:, :D], (1,), (0,)) + querybias_full).astype(bf16).reshape(S, R, D)
    gating = jax.nn.sigmoid(mm(pre, proj_full[:, D : 2 * D], (1,), (0,)))

    probs, attended = attention(query, kv, bias_all, mask_add)
    attended = attended.reshape(S * R, D)

    adapt_own = mm(cond_low, cond_rest, (1,), (1,)) + jnp.concatenate([o[1], o[2], sh[1], o[3]], axis=1)
    pregate, postscale, postshift, postgate = jnp.split(adapt_own, 4, axis=-1)
    expand_full = pinned(jnp.concatenate([rows_of(second_all, i * pr, pr) for i in range(4)], axis=1))
    comb_full = rows_of(second_all, 4 * pr, pr)
    reduce_full = rows_of(second_all, 5 * pr, rr)

    gated = (gating * attended).astype(bf16)
    branch = mm(gated, comb_full, (1,), (0,))
    pregate_sig = jax.nn.sigmoid(pregate)
    residual = tokens + pregate_sig * branch
    post_norm, post_inv = normal_rows(residual)
    post_gain = jax.nn.sigmoid(postscale)
    posthidden = (post_gain * post_norm + postshift).astype(bf16)
    upgate = mm(posthidden, expand_full, (1,), (0,))
    FF = upgate.shape[-1] // 2
    preact, upper = upgate[:, :FF], upgate[:, FF:]
    preact_sig = jax.nn.sigmoid(preact)
    swished = preact * preact_sig
    activated = (swished * upper).astype(bf16)
    trans = lax.optimization_barrier(mm(activated, reduce_full, (1,), (0,)))
    postgate_sig = jax.nn.sigmoid(postgate)
    mixed = (residual + postgate_sig * trans).astype(bf16)

    def owned(grad):
        return [g.reshape(G, T, g.shape[0] // W, D) for g in blocks(grad)]

    g_out = cotangent.reshape(S * R, D)
    trans_back = (postgate_sig * g_out).astype(bf16)
    postgate_back = g_out * trans * slope(postgate_sig)
    reducer_part = mm(activated, trans_back, (0,), (0,), bf16)
    act_back = mm(trans_back, reduce_full, (1,), (1,))
    up_back = jnp.concatenate(
        [act_back * upper * preact_sig * (1.0 + preact * (1.0 - preact_sig)), act_back * swished], axis=-1
    ).astype(bf16)
    expander_part = mm(posthidden, up_back, (0,), (0,), bf16)
    posthidden_back = mm(up_back, expand_full, (1,), (1,))
    postscale_back = posthidden_back * post_norm * slope(post_gain)
    residual_back = g_out + norm_back(post_norm, post_inv, posthidden_back * post_gain)
    branch_back = (pregate_sig * residual_back).astype(bf16)
    pregate_back = residual_back * branch * slope(pregate_sig)
    combiner_part = mm(gated, branch_back, (0,), (0,), bf16)
    gated_back = mm(branch_back, comb_full, (1,), (1,))
    gating_low = (attended * gated_back * slope(gating)).astype(bf16)
    gate_part = mm(pre, gating_low, (0,), (0,), bf16)
    second_part = jnp.concatenate(
        owned(expander_part) + owned(combiner_part) + owned(reducer_part) + owned(gate_part), axis=2
    )
    second_owned = pinned(second_part.reshape(G, -1, D))
    second_part = lax.psum_scatter(second_owned, "samp", scatter_dimension=0, tiled=False)

    attended_back = (gating * gated_back).astype(bf16)
    query_back, dkv, *bias_back = attention_back(
        me.astype(jnp.int32)[None], probs, attended_back.reshape(S, R, D), kv, query, second_owned, fold, G
    )
    query_back = query_back.reshape(S * R, D)
    dkv = dkv.reshape(S, 2 * D, N)

    later = jnp.concatenate([pregate_back, postscale_back, posthidden_back, postgate_back], axis=-1)
    later_sums = jnp.split(jnp.sum(later, axis=0), 4)
    later_low = later.astype(bf16)
    later_part = mm(later_low, cond_low, (0,), (0,), bf16)
    later_back = mm(later_low, cond_rest, (1,), (0,))

    pre_back_all = pinned(mm(dkv, proj_full[:, 2 * D :], (1,), (1,), bf16))
    if fold > 1:
        kept, given = bias_back
        bias_both = (kept.astype(f32) + hop(given, "samp", 1).astype(f32) + zero(pre_back_all).astype(f32)).astype(bf16)
        bias_sum = sum_samp_end(bias_both)
    else:
        bias_sum = sum_samp([bias_back[0].reshape(H * R, G, C).transpose(1, 0, 2)]).reshape(H, R, C)
    qg_low = jnp.concatenate([query_back.astype(bf16), gating_low], axis=-1)
    q_part = mm(pre, query_back.astype(bf16), (0,), (0,), bf16)
    kv_part = mm(pre_all.reshape(S, N, D), dkv, (0, 1), (0, 2), bf16)
    proj_owned = pinned(jnp.concatenate(owned(q_part) + owned(kv_part), axis=2).reshape(G, -1, D))
    proj_part = lax.psum_scatter(proj_owned, "samp", scatter_dimension=0, tiled=False)
    parts = sum_tok(pre_back_all.reshape(S, T, R, D), dim=1, apart=True)
    parts = [mm(qg_low, proj_full[:, : 2 * D], (1,), (1,))] + [p.reshape(S * R, D) for p in parts]
    tokens_grad, early_sums, early_part, singles_part, sample_sums = finish(
        parts, tokens_in.reshape(S * R, D), own(gain_all), residual_back, later_back, cond, cond_low, cond_pre,
        [proj_owned, bias_both if fold > 1 else bias_sum], S,
    )
    pair_grad, pairhead_part = pair_back(pairwise[0], bias_sum.transpose(1, 0, 2), pht, early_part, fold)
    offsets_part = jnp.concatenate([early_sums[0], later_sums[0], later_sums[1], later_sums[3]])
    shifts_part = jnp.concatenate([early_sums[1], later_sums[2]])
    querybias_part = jnp.sum(query_back, axis=0)
    cond_part = pinned(jnp.concatenate([early_part, later_part], axis=0).reshape(G, T * cc, CS))
    vec_part = jnp.concatenate(
        [offsets_part.reshape(G, T, no), shifts_part.reshape(G, T, ns), querybias_part.reshape(G, T, pr)], axis=-1
    )
    vec_part = jnp.zeros((G, T, 8, CS), bf16).at[:, :, 0, : vec.shape[0]].set(vec_part.astype(bf16))
    vec_part = pinned(vec_part.reshape(G, T * 8, CS))
    cs = CS // G
    extra = singles_part.reshape(G, cs, CS)
    extra = pinned(extra)
    cond_both = sum_samp_start([cond_part, vec_part, extra], bias_sum)
    second_part, proj_part = second_part.reshape(T, -1, D), proj_part.reshape(T, -1, D)
    both_part = jnp.concatenate([second_part + zero(cond_part).astype(bf16), proj_part], axis=1)
    both_sum = lax.psum_scatter(both_part, "tok", scatter_dimension=0, tiled=False).astype(f32)
    second_sum, proj_sum = both_sum[: second.shape[0]], both_sum[second.shape[0] :]
    both = sum_samp_end(cond_both)
    cond_half = jnp.concatenate([both[: T * cc].reshape(T, cc, CS), both[T * cc : T * (cc + 8)].reshape(T, 8, CS)], axis=1)
    singles_t = both[T * (cc + 8) :, :R]

    by_sample = jnp.concatenate(
        [sample_sums[:S], jnp.broadcast_to(jnp.where(t == 0, noise_level, 0)[:, None], (S, 128)).astype(f32)],
        axis=1,
    )
    placed = lax.dynamic_update_slice_in_dim(jnp.zeros((G * S, CS + 128), f32), by_sample, me * S, 0)
    small = everyone(jnp.concatenate([placed, jnp.pad(pairhead_part, ((0, 0), (0, CS)))], axis=0), cond_half)
    level_all = small[: G * S, CS].astype(jnp.int32)
    levels = jnp.arange(noise_table.shape[0], dtype=jnp.int32)
    level_hot = (levels[:, None] == level_all[None, :]).astype(f32)
    noise_grad = jnp.dot(level_hot, small[: G * S, :CS], precision=lax.Precision.HIGHEST)
    pairhead_grad = small[G * S :, : pairhead_part.shape[1]].T

    def unblocks(x, order):
        return jnp.concatenate([x[i * pr : (i + 1) * pr] for i in order], axis=1)

    cond_sum = sum_tok(cond_half.astype(bf16), small)
    cond_out, vec_out = cond_sum[:cc], cond_sum[cc]
    return (
        mixed.reshape(S, R, D),
        tokens_grad.reshape(S, R, D),
        singles_t.T[None],
        pair_grad[None],
        noise_grad,
        cond_out.T,
        vec_out[:no],
        vec_out[no : no + ns],
        unblocks(proj_sum, (1, 2, 3, 0)),
        vec_out[no + ns : no + ns + pr],
        second_sum[4 * pr : 5 * pr],
        unblocks(second_sum, (0, 1, 2, 3)),
        second_sum[5 * pr :],
        pairhead_grad,
    )


def solution(mesh):
    shard = ("samp", "tok")
    in_specs = (
        P("samp", "tok", None), P("samp", "tok", None), P(None, "tok", None), P(), P("samp"), P(),
        P(None, "tok", "samp", None), P(None, shard), P(shard), P(shard), P(shard, None), P(shard),
        P(shard, None), P(shard, None), P(shard, None), P(),
    )
    out_specs = (
        P("samp", "tok", None), P("samp", "tok", None), P(None, "tok", "samp"), P(None, "tok", "samp", None), P(),
        P(None, shard), P(shard), P(shard), P(shard, None), P(shard), P(shard, None), P(shard, None),
        P(shard, None), P(),
    )
    return jax.shard_map(per_device, mesh=mesh, in_specs=in_specs, out_specs=out_specs, check_vma=False)
```

```python
from jax.experimental.layout import Layout, with_layout_constraint
import jax
import jax.numpy as jnp
from jax import lax
from jax.experimental import pallas as pl
from jax.experimental.pallas import tpu as pltpu
from jax.sharding import PartitionSpec as P

DH = 48
EPS = 1e-5
WIN = 256
ROWS = 32
VMEM_BYTES = 56 * 1024 * 1024
f32 = jnp.float32
bf16 = jnp.bfloat16
COST = pl.CostEstimate(flops=1024, bytes_accessed=1024, transcendentals=0)
NT = (((1,), (1,)), ((), ()))
TN = (((0,), (0,)), ((), ()))


def params():
    return pltpu.CompilerParams(vmem_limit_bytes=VMEM_BYTES)


def window(h, width):
    w = pl.multiple_of(jnp.minimum((h * DH) // 128 * 128, width - WIN), 128)
    lane = lax.broadcasted_iota(jnp.int32, (1, WIN), 1) + w
    return w, (lane >= h * DH) & (lane < h * DH + DH)


def attention_body(q_ref, k_ref, v_ref, bias_ref, mask_ref, p_ref, att_ref, scores):
    samples, rows, width = q_ref.shape
    heads = bias_ref.shape[0]
    mask = mask_ref[...]
    windows = [window(pl.program_id(0) * heads + u, width) for u in range(heads)]
    for u, (w, inside) in enumerate(windows):
        for b in range(samples):
            q = jnp.where(inside, q_ref[b, :, pl.ds(w, WIN)], 0)
            scores[u * samples + b] = lax.dot_general(q, k_ref[b, :, pl.ds(w, WIN)], NT, preferred_element_type=f32)
    for u in range(heads):
        for i in range(0, rows, ROWS):
            bias = bias_ref[u, i : i + ROWS].astype(f32) + mask
            for b in range(samples):
                s = scores[u * samples + b, i : i + ROWS] * (DH ** -0.5) + bias
                e = jnp.exp(s - jnp.max(s, axis=1, keepdims=True))
                p_ref[u, b, i : i + ROWS] = (e * (1.0 / jnp.sum(e, axis=1, keepdims=True))).astype(bf16)
    for u, (w, inside) in enumerate(windows):
        for b in range(samples):
            o = jnp.dot(p_ref[u, b], v_ref[b, :, pl.ds(w, WIN)], preferred_element_type=f32)
            att_ref[b, :, pl.ds(w, WIN)] = jnp.where(inside, o, att_ref[b, :, pl.ds(w, WIN)])


def attention(q, kv, bias, mask):
    S, R, D = q.shape
    N, H = kv.shape[1], bias.shape[0]
    heads = 4

    def whole(*shape):
        return pl.BlockSpec(shape, lambda h: (0,) * len(shape))

    return pl.pallas_call(
        attention_body,
        grid=(H // heads,),
        in_specs=[
            whole(S, R, D),
            whole(S, N, D),
            pl.BlockSpec((S, N, D), lambda h: (0, 0, 1)),
            pl.BlockSpec((heads, R, N), lambda h: (h, 0, 0)),
            whole(1, N),
        ],
        out_specs=[pl.BlockSpec((heads, S, R, N), lambda h: (h, 0, 0, 0)), whole(S, R, D)],
        out_shape=[jax.ShapeDtypeStruct((H, S, R, N), bf16), jax.ShapeDtypeStruct((S, R, D), f32)],
        scratch_shapes=[pltpu.VMEM((heads * S, R, N), f32)],
        compiler_params=params(),
        cost_estimate=COST,
        name="attention",
    )(q, kv, kv, bias, mask)


def attention_back_body(fold, me_ref, p_ref, do_ref, k_ref, v_ref, q_ref, dq_ref, dkv_ref, *rest):
    *bb_refs, qt, dot_, dp_all, low_all, acc = rest
    samples, rows, width = do_ref.shape
    heads = p_ref.shape[0]
    step = pl.program_id(0)

    @pl.when(step == 0)
    def _():
        for b in range(samples):
            qt[b] = q_ref[b].astype(f32).T.astype(bf16)
            dot_[b] = do_ref[b].astype(f32).T.astype(bf16)

    windows = [window(step * heads + u, width) for u in range(heads)]
    for u, (w, inside) in enumerate(windows):
        for b in range(samples):
            do = jnp.where(inside, do_ref[b, :, pl.ds(w, WIN)], 0)
            dp_all[u * samples + b] = lax.dot_general(do, v_ref[b, :, pl.ds(w, WIN)], NT, preferred_element_type=f32)
    for u in range(heads):
        for i in range(0, rows, ROWS):
            total = None
            for b in range(samples):
                dp = dp_all[u * samples + b, i : i + ROWS]
                p = p_ref[u, b, i : i + ROWS].astype(f32)
                ds = p * (dp - jnp.sum(p * dp, axis=1, keepdims=True))
                low_all[u * samples + b, i : i + ROWS] = ds.astype(bf16)
                total = ds if total is None else total + ds
            acc[u, i : i + ROWS] = total
    for u, (w, inside) in enumerate(windows):
        own = pl.ds(pl.multiple_of((step * heads + u) * DH, 16), DH)
        for b in range(samples):
            low = low_all[u * samples + b]
            dq = jnp.dot(low, k_ref[b, :, pl.ds(w, WIN)], preferred_element_type=f32) * (DH ** -0.5)
            dq_ref[b, :, pl.ds(w, WIN)] = jnp.where(inside, dq, dq_ref[b, :, pl.ds(w, WIN)])
            dk = jnp.dot(qt[b, own, :], low, preferred_element_type=f32) * (DH ** -0.5)
            dv = jnp.dot(dot_[b, own, :], p_ref[u, b], preferred_element_type=f32)
            dkv_ref[b, 0, u * DH : (u + 1) * DH] = dk.astype(bf16)
            dkv_ref[b, 1, u * DH : (u + 1) * DH] = dv.astype(bf16)
        if fold == 1:
            bb_refs[0][u] = acc[u].astype(bf16)
            continue
        kept_ref, given_ref = bb_refs
        count, _, part, lanes = kept_ref.shape
        c = lanes // fold
        odd = me_ref[0] % 2 == 1

        def piece(s):
            return jnp.concatenate(
                [acc[u, i * part : (i + 1) * part, s * c : (s + 1) * c] for i in range(fold)], axis=1
            )

        for j in range(count):
            first, second = piece(2 * j), piece(2 * j + 1)
            kept_ref[j, u] = jnp.where(odd, second, first).astype(bf16)
            given_ref[j, u] = jnp.where(odd, first, second).astype(bf16)


def attention_back(me, p, do, kv, q, first, fold, groups):
    H, S, R, N = p.shape
    D = do.shape[2]
    heads = 2

    def whole(*shape):
        return pl.BlockSpec(shape, lambda h, m: (0,) * len(shape))

    if fold == 1:
        bb_specs, bb_shapes = [pl.BlockSpec((heads, R, N), lambda h, m: (h, 0, 0))], [(H, R, N)]
    else:
        tail = (R // fold, fold * (N // groups))
        bb_specs = [pl.BlockSpec((groups // 2, heads) + tail, lambda h, m: (0, h, 0, 0))] * 2
        bb_shapes = [(groups // 2, H) + tail] * 2

    def body(me_ref, p_ref, do_ref, k_ref, v_ref, q_ref, _, *refs):
        attention_back_body(fold, me_ref, p_ref, do_ref, k_ref, v_ref, q_ref, *refs)

    return pl.pallas_call(
        body,
        grid_spec=pltpu.PrefetchScalarGridSpec(
            num_scalar_prefetch=1,
            grid=(H // heads,),
            in_specs=[
                pl.BlockSpec((heads, S, R, N), lambda h, m: (h, 0, 0, 0)),
                whole(S, R, D),
                whole(S, N, D),
                pl.BlockSpec((S, N, D), lambda h, m: (0, 0, 1)),
                whole(S, R, D),
                pl.BlockSpec(memory_space=pl.ANY),
            ],
            out_specs=[whole(S, R, D), pl.BlockSpec((S, 2, heads * DH, N), lambda h, m: (0, 0, h, 0))] + bb_specs,
            scratch_shapes=[
                pltpu.VMEM((S, D, R), bf16),
                pltpu.VMEM((S, D, R), bf16),
                pltpu.VMEM((heads * S, R, N), f32),
                pltpu.VMEM((heads * S, R, N), bf16),
                pltpu.VMEM((heads, R, N), f32),
            ],
        ),
        out_shape=[
            jax.ShapeDtypeStruct((S, R, D), f32),
            jax.ShapeDtypeStruct((S, 2, D, N), bf16),
        ]
        + [jax.ShapeDtypeStruct(shape, bf16) for shape in bb_shapes],
        compiler_params=params(),
        cost_estimate=COST,
        name="attention_back",
    )(me, p, do, kv, kv, q, first)


def normal_rows(x):
    c = x - jnp.mean(x, axis=-1, keepdims=True)
    r = lax.rsqrt(jnp.mean(c * c, axis=-1, keepdims=True) + EPS)
    return c * r, r


def split(x):
    hi = x.astype(bf16)
    return hi, (x - hi.astype(f32)).astype(bf16)


def lane_mean(x):
    ones = jnp.full((x.shape[1], x.shape[1]), 1.0, bf16)
    hi, lo = split(x)
    total = jnp.dot(hi, ones, preferred_element_type=f32) + jnp.dot(lo, ones, preferred_element_type=f32)
    return total * (1.0 / x.shape[1])


def pair_bias_body(x_ref, ph_ref, out_ref, buf):
    fold, n, C, E = x_ref.shape
    ph = ph_ref[...]
    for i in range(n):
        x = x_ref[:, i].reshape(fold * C, E) if fold > 1 else x_ref[0, i]
        nrm, _ = normal_rows(x.astype(f32))
        buf[:, i, :] = lax.dot_general(ph, nrm.astype(bf16), NT, preferred_element_type=f32)
    out_ref[...] = buf[...].astype(bf16)


def pair_bias(x, pht, fold):
    R, C, E = x.shape
    H = pht.shape[0]
    rows = R // fold
    blk = 16
    return pl.pallas_call(
        pair_bias_body,
        grid=(rows // blk,),
        in_specs=[
            pl.BlockSpec((fold, blk, C, E), lambda i: (0, i, 0, 0)), pl.BlockSpec((H, E), lambda i: (0, 0)),
        ],
        out_specs=pl.BlockSpec((H, blk, fold * C), lambda i: (0, i, 0)),
        out_shape=jax.ShapeDtypeStruct((H, rows, fold * C), bf16),
        scratch_shapes=[pltpu.VMEM((H, blk, fold * C), f32)],
        compiler_params=params(),
        cost_estimate=COST,
        name="pair_bias",
    )(x.reshape(fold, rows, C, E), pht)


def pair_back_body(x_ref, bb_ref, ph_ref, _, out_ref, dph_ref):
    fold, n, C, E = x_ref.shape
    H = ph_ref.shape[0]
    ph = ph_ref[...].astype(f32)
    ph_hi, ph_lo = split(ph - jnp.mean(ph, axis=-1, keepdims=True))
    ph4 = jnp.concatenate([ph_hi, ph_lo, ph_hi, ph_lo], axis=0)
    acc = jnp.zeros((2 * H, E), f32)
    for i in range(n):
        x = x_ref[:, i].reshape(fold * C, E) if fold > 1 else x_ref[0, i]
        nrm, r = normal_rows(x.astype(f32))
        hi, lo = split(bb_ref[i])
        g = lax.dot_general(
            jnp.concatenate([hi, hi, lo, lo], axis=0), ph4, TN, preferred_element_type=f32
        )
        grad = r * (g - nrm * lane_mean(g * nrm))
        if fold > 1:
            out_ref[:, i] = grad.reshape(fold, C, E)
        else:
            out_ref[0, i] = grad
        acc += jnp.dot(jnp.concatenate([hi, lo], axis=0), nrm.astype(bf16), preferred_element_type=f32)
    part = acc[:H] + acc[H:]

    @pl.when(pl.program_id(0) == 0)
    def _():
        dph_ref[...] = part

    @pl.when(pl.program_id(0) != 0)
    def _():
        dph_ref[...] += part


def pair_back(x, bb, pht, first, fold):
    R, C, E = x.shape
    H = pht.shape[0]
    rows = R // fold
    blk = 8
    grad, dph = pl.pallas_call(
        pair_back_body,
        grid=(rows // blk,),
        in_specs=[
            pl.BlockSpec((fold, blk, C, E), lambda i: (0, i, 0, 0)),
            pl.BlockSpec((blk, H, fold * C), lambda i: (i, 0, 0)),
            pl.BlockSpec((H, E), lambda i: (0, 0)),
            pl.BlockSpec(memory_space=pl.ANY),
        ],
        out_specs=[pl.BlockSpec((fold, blk, C, E), lambda i: (0, i, 0, 0)), pl.BlockSpec((H, E), lambda i: (0, 0))],
        out_shape=[jax.ShapeDtypeStruct((fold, rows, C, E), f32), jax.ShapeDtypeStruct((H, E), f32)],
        compiler_params=params(),
        cost_estimate=COST,
        name="pair_back",
    )(x.reshape(fold, rows, C, E), bb, pht, first)
    return grad.reshape(R, C, E), dph


def lay_bias_body(me_ref, *refs):
    pieces, (out_ref, slots, sems) = refs[:-3], refs[-3:]
    h = pl.program_id(0)
    part, lanes = slots.shape[2:]
    fold = out_ref.shape[1] // part
    c = lanes // fold

    @pl.when(h == 0)
    def _():
        copies = [
            pltpu.make_async_copy(p, slots.at[jnp.bitwise_xor(me_ref[0], k)], sems.at[k]) for k, p in enumerate(pieces)
        ]
        for copy in copies:
            copy.start()
        for copy in copies:
            copy.wait()

    laid = [slots[s, h].astype(f32) for s in range(len(pieces))]
    for i in range(fold):
        out_ref[0, i * part : (i + 1) * part, :] = jnp.concatenate(
            [p[:, i * c : (i + 1) * c] for p in laid], axis=1
        ).astype(bf16)


def lay_bias(me, pieces, rows):
    H, part, lanes = pieces[0].shape
    count = len(pieces)
    keys = count * lanes // (rows // part)
    return pl.pallas_call(
        lay_bias_body,
        grid_spec=pltpu.PrefetchScalarGridSpec(
            num_scalar_prefetch=1,
            grid=(H,),
            in_specs=[pl.BlockSpec(memory_space=pl.ANY)] * count,
            out_specs=pl.BlockSpec((1, rows, keys), lambda h, s: (h, 0, 0)),
            scratch_shapes=[pltpu.VMEM((count, H, part, lanes), bf16), pltpu.SemaphoreType.DMA((count,))],
        ),
        out_shape=jax.ShapeDtypeStruct((H, rows, keys), bf16),
        compiler_params=params(),
        cost_estimate=COST,
        name="lay_bias",
    )(me, *pieces)


def lay_vectors_body(counts, x_ref, out_ref):
    x = x_ref[...]
    D = out_ref.shape[1]
    row = start = 0
    for n in counts:
        per = D // n
        for i in range(x.shape[0] // per):
            pieces = [x[j : j + 1, start : start + n] for j in range(i * per, (i + 1) * per)]
            out_ref[row : row + 1, :] = jnp.concatenate(pieces, axis=1)
            row += 1
        start += n
    out_ref[row:, :] = jnp.zeros((out_ref.shape[0] - row, D), f32)


def lay_vectors(x, *counts):
    D = x.shape[1]

    def body(x_ref, out_ref):
        lay_vectors_body(counts, x_ref, out_ref)

    return pl.pallas_call(
        body,
        out_shape=jax.ShapeDtypeStruct((8, D), f32),
        compiler_params=params(),
        cost_estimate=COST,
        name="lay_vectors",
    )(x)


def center(n, r, g):
    return r * (g - jnp.mean(g, axis=-1, keepdims=True) - n * jnp.mean(g * n, axis=-1, keepdims=True))


def finish(parts, tokens, gain, residual_back, later_back, cond, cond_low, cond_pre, first, samples):
    rows, D = tokens.shape
    CS = cond.shape[1]
    count = len(parts)

    def body(*refs):
        x = refs[0][...].astype(f32)
        for p in refs[1:count]:
            x = x + p[...].astype(f32)
        tok, gain_ref, resid, later, cond_ref, low_ref, pre_ref = refs[count : count + 7]
        grad, sums, part, single, by_sample = refs[count + 7 + len(first) :]
        n, r = normal_rows(tok[...].astype(f32))
        g = gain_ref[...]
        scale = x * n * (g * (1.0 - g))
        grad[...] = resid[...] + center(n, r, x * g)
        sums[...] = jnp.zeros_like(sums)
        sums[0:1, :] = jnp.sum(scale, axis=0, keepdims=True)
        sums[1:2, :] = jnp.sum(x, axis=0, keepdims=True)
        early = jnp.concatenate([scale.astype(bf16), x.astype(bf16)], axis=1)
        part[...] = lax.dot_general(early, low_ref[...], TN, preferred_element_type=f32).astype(bf16)
        back = later[...] + jnp.dot(early, pre_ref[...], preferred_element_type=f32)
        cond_grad = center(*normal_rows(cond_ref[...]), back)
        each = rows // samples
        total = cond_grad[:each]
        for b in range(1, samples):
            total = total + cond_grad[b * each : (b + 1) * each]
        single[...] = jnp.concatenate([total.T, jnp.zeros((CS, CS - each), f32)], axis=1).astype(bf16)
        by_sample[...] = jnp.zeros_like(by_sample)
        for b in range(samples):
            by_sample[b : b + 1, :] = jnp.sum(cond_grad[b * each : (b + 1) * each], axis=0, keepdims=True)

    shapes = [(rows, D), (8, D), (2 * D, CS), (CS, CS), (8, CS)]
    kinds = [f32, f32, bf16, bf16, f32]
    vmem = pl.BlockSpec(memory_space=pltpu.VMEM)
    return pl.pallas_call(
        body,
        in_specs=[vmem] * (count + 7) + [pl.BlockSpec(memory_space=pl.ANY)] * len(first),
        out_specs=[vmem] * 5,
        out_shape=[jax.ShapeDtypeStruct(s, kind) for s, kind in zip(shapes, kinds)],
        compiler_params=params(),
        cost_estimate=COST,
        name="finish",
    )(*parts, tokens, gain, residual_back, later_back, cond, cond_low, cond_pre, *first)


def pinned(x):
    return with_layout_constraint(x, Layout(major_to_minor=tuple(range(x.ndim))))


def norm_back(n, r, g):
    return r * (g - jnp.mean(g, axis=-1, keepdims=True) - n * jnp.mean(g * n, axis=-1, keepdims=True))


def slope(s):
    return s * (1.0 - s)


def mm(a, b, ca, cb, out=f32):
    return lax.dot_general(a, b, ((ca, cb), ((), ())), preferred_element_type=f32).astype(out)


def hop(x, axis, k):
    return lax.ppermute(x, axis, [(i, i ^ k) for i in range(lax.axis_size(axis))])


def at(x, i):
    return lax.dynamic_index_in_dim(x, i, 0, keepdims=False)


def everyone(x, *others):
    steps = [(axis, 1 << i) for axis in ("tok", "samp") for i in range((lax.axis_size(axis) - 1).bit_length())]
    for i, (axis, k) in enumerate(steps):
        x = x + hop(x, axis, k)
        if i == 0:
            x = x + zero(*others).astype(f32)
    return x


def zero(*others):
    corners = [lax.slice(o, (0,) * o.ndim, (1,) * o.ndim).reshape(()).astype(f32) for o in others]
    return sum((jnp.abs(c) > 1e30).astype(jnp.int32) for c in corners)


def gather_tok(parts, others):
    n, t = lax.axis_size("tok"), lax.axis_index("tok")
    width = parts[0][0].shape[-1]
    rows = [p.size // width for p, _ in parts]
    x = jnp.concatenate([p.reshape(-1, width) for p, _ in parts], axis=0)
    up, down = [x], [x]
    for _ in range(1, n):
        up.append(lax.ppermute(up[-1], "tok", [(i, i + 1) for i in range(n - 1)]))
        down.append(lax.ppermute(down[-1], "tok", [(i + 1, i) for i in range(n - 1)]))
    outs, start = [], 0
    for i, ((p, dim), count) in enumerate(zip(parts, rows)):
        place = t + n + zero(*others[i])
        out = jnp.zeros(p.shape[:dim] + (n,) + p.shape[dim:], p.dtype)
        for k in range(n):
            got = [u[start : start + count].reshape(p.shape) for u in (up[k], down[n - k if k else 0])]
            got = got[0] if k == 0 else jnp.where(t >= k, *got)
            out = lax.dynamic_update_slice_in_dim(out, jnp.expand_dims(got, dim), (place - k) % n, dim)
        outs.append(out)
        start += count
    return outs


def sum_tok(x, *others, dim=0, apart=False):
    n, t = lax.axis_size("tok"), lax.axis_index("tok")
    x = x.reshape(x.shape[:dim] + (n // 2, 2) + x.shape[dim + 1 :])

    def part(v, i, d):
        return lax.dynamic_index_in_dim(v, i, d, keepdims=False)

    came = hop(part(x, 1 - t % 2, dim + 1), "tok", 1)
    pair = part(x, t % 2, dim + 1).astype(f32) + came.astype(f32)
    given = [hop(part(pair, (t // 2) ^ k, dim).astype(bf16), "tok", 2 * k) for k in range(1, n // 2)]
    total = part(pair, t // 2 + (zero(*others) if others else 0), dim)
    if apart:
        return [total] + given
    for g in given:
        total = total + g.astype(f32)
    return total


def sum_samp_start(parts, *others):
    n = lax.axis_size("samp")
    if n != 8:
        return jnp.concatenate([p.astype(bf16) for p in parts], axis=-2)
    c = lax.axis_index("samp") % 2

    def half(which):
        picked = [
            lax.dynamic_index_in_dim(p.reshape((n // 2, 2) + p.shape[1:]), which, 1, keepdims=False) for p in parts
        ]
        return jnp.concatenate(picked, axis=-2) if len(picked) > 1 else picked[0]

    other = hop(half(1 - c).astype(bf16), "samp", 1)
    both = half(c + zero(*others)).astype(f32) + other.astype(f32)
    return pinned(both.astype(bf16))


def sum_samp_end(both):
    n = lax.axis_size("samp")
    if n != 8:
        return lax.psum_scatter(both, "samp", scatter_dimension=0, tiled=False).astype(f32)
    j = lax.axis_index("samp") // 2
    total = at(both, j).astype(f32)
    for k in range(1, n // 2):
        total = total + hop(at(both, j ^ k), "samp", 2 * k).astype(f32)
    return total


def sum_samp(parts):
    return sum_samp_end(sum_samp_start(parts))


def per_device(
    tokens_in, cotangent, singles, noise_table, noise_level, pad_mask, pairwise, conditioner,
    offsets, shifts, projector, querybias, combiner, expander, reducer, pairhead,
):
    S, R, D = tokens_in.shape
    C = pairwise.shape[2]
    N = pad_mask.shape[1]
    H = pairhead.shape[1]
    CS = conditioner.shape[0]
    T, G = lax.axis_size("tok"), lax.axis_size("samp")
    W = G * T
    t, me = lax.axis_index("tok"), lax.axis_index("samp")
    fold = 4 if G == 8 else 1

    def blocks(w):
        return [w[:, i * D : (i + 1) * D] for i in range(w.shape[1] // D)]

    def rows_of(buf, start, count):
        return buf[:, start : start + count].reshape(W * count, D)

    cond_t = conditioner.T
    cc, pr, rr = cond_t.shape[0], projector.shape[0], reducer.shape[0]
    no, ns = offsets.shape[0], shifts.shape[0]
    vec = jnp.concatenate([offsets, shifts, querybias])
    vec_row = jnp.zeros((8, D), bf16).at[0, : vec.shape[0]].set(vec)
    cond_rows = jnp.concatenate([cond_t[: cc // 2], cond_t[cc // 2 :]], axis=1)
    q_block, k_block, v_block, g_block = blocks(projector)
    mine = lax.dynamic_slice_in_dim(singles[0], me * (R // G), R // G, 0)
    if R % (2 * G) == 0:
        single = jnp.concatenate([mine[: R // G // 2], mine[R // G // 2 :]], axis=1)
    else:
        single = jnp.pad(mine, ((0, 0), (0, D - CS)))
    single_rows = single.shape[0]
    first = jnp.concatenate([q_block, g_block, k_block, v_block, cond_rows, vec_row, single], axis=0)
    second = jnp.concatenate(blocks(expander) + [combiner, reducer], axis=0)
    first_all = lax.all_gather(first, ("samp", "tok"), axis=0)

    pht = pairhead.T
    piece = pair_bias(pairwise[0], pht, fold)
    if fold > 1:
        even = [piece] + [hop(piece, "samp", k) for k in range(2, G, 2)]
        pieces = [p for e in even for p in (e, hop(e, "samp", 1))]
        bias_all = lay_bias(me.astype(jnp.int32)[None], pieces, R)
    else:
        bias_all = jnp.transpose(lax.all_gather(piece, "samp", axis=0), (1, 2, 0, 3)).reshape(H, R, N)
    mask_add = (pad_mask.astype(f32) - 1.0) * 1e9
    ready = lax.dynamic_index_in_dim(first_all, zero(bias_all), 0)
    tokens_all, second_mine = gather_tok([(tokens_in, 1), (second, 0)], [[bias_all], [ready]])
    second_all = lax.all_gather(second_mine, "samp", axis=0).reshape(W, second.shape[0], D)

    tokens_all = tokens_all.reshape(S * N, D)
    token_norm_all, _ = normal_rows(tokens_all.astype(f32))
    singles_all = first_all[:, -single_rows:].reshape(G, T, single_rows, D).transpose(1, 0, 2, 3)
    if single_rows * 2 == R // G:
        halves = [singles_all[:, :, :, :CS], singles_all[:, :, :, CS:]]
        singles_all = jnp.concatenate(halves, axis=2).reshape(N, CS)
    else:
        singles_all = singles_all[:, :, :, :CS].reshape(N, CS)
    levels = jnp.arange(noise_table.shape[0], dtype=jnp.int32)
    noise_rows = jnp.dot(
        (noise_level[:, None] == levels[None, :]).astype(f32), noise_table, precision=lax.Precision.HIGHEST
    )
    cond_all, _ = normal_rows((singles_all.astype(f32)[None] + noise_rows[:, None]).reshape(S * N, CS))
    cond_low_all = cond_all.astype(bf16)
    cond = (singles.astype(f32) + noise_rows[:, None]).reshape(S * R, CS)
    cond_low = normal_rows(cond)[0].astype(bf16)
    tokens = tokens_in.reshape(S * R, D).astype(f32)

    def own(x):
        return lax.dynamic_slice_in_dim(x.reshape(S, N, x.shape[-1]), t * R, R, 1).reshape(S * R, x.shape[-1])

    proj_full = jnp.concatenate([rows_of(first_all, i * pr, pr) for i in range(4)], axis=1)
    def cond_rows_of(start, stop):
        a, b = start // cc, -(-stop // cc)
        part = first_all[a:b, 4 * pr : 4 * pr + cc // 2]
        part = jnp.concatenate([part[:, :, :CS], part[:, :, CS:]], axis=1).reshape((b - a) * cc, CS)
        return part[start - a * cc : stop - a * cc]

    cond_pre, cond_rest = cond_rows_of(0, 2 * D), cond_rows_of(2 * D, 6 * D)
    vecs = first_all[:, 4 * pr + cc // 2].astype(f32)
    if fold > 1:
        rows = lay_vectors(vecs, no, ns, pr)
        o, sh, querybias_full = [rows[i : i + 1] for i in range(4)], [rows[4:5], rows[5:6]], rows[6:7]
    else:
        o = jnp.split(vecs[:, :no].reshape(1, W * no), 4, axis=1)
        sh = jnp.split(vecs[:, no : no + ns].reshape(1, W * ns), 2, axis=1)
        querybias_full = vecs[:, no + ns : no + ns + pr].reshape(1, W * pr)

    adapt_pre = mm(cond_low_all, cond_pre, (1,), (1,)) + jnp.concatenate([o[0], sh[0]], axis=1)
    gain_all = jax.nn.sigmoid(adapt_pre[:, :D])
    pre_all = (gain_all * token_norm_all + adapt_pre[:, D:]).astype(bf16)
    pre = own(pre_all)
    kv = mm(pre_all, proj_full[:, 2 * D :], (1,), (0,), bf16).reshape(S, N, 2 * D)
    query = (mm(pre, proj_full[:, :D], (1,), (0,)) + querybias_full).astype(bf16).reshape(S, R, D)
    gating = jax.nn.sigmoid(mm(pre, proj_full[:, D : 2 * D], (1,), (0,)))

    probs, attended = attention(query, kv, bias_all, mask_add)
    attended = attended.reshape(S * R, D)

    adapt_own = mm(cond_low, cond_rest, (1,), (1,)) + jnp.concatenate([o[1], o[2], sh[1], o[3]], axis=1)
    pregate, postscale, postshift, postgate = jnp.split(adapt_own, 4, axis=-1)
    expand_full = pinned(jnp.concatenate([rows_of(second_all, i * pr, pr) for i in range(4)], axis=1))
    comb_full = rows_of(second_all, 4 * pr, pr)
    reduce_full = rows_of(second_all, 5 * pr, rr)

    gated = (gating * attended).astype(bf16)
    branch = mm(gated, comb_full, (1,), (0,))
    pregate_sig = jax.nn.sigmoid(pregate)
    residual = tokens + pregate_sig * branch
    post_norm, post_inv = normal_rows(residual)
    post_gain = jax.nn.sigmoid(postscale)
    posthidden = (post_gain * post_norm + postshift).astype(bf16)
    upgate = mm(posthidden, expand_full, (1,), (0,))
    FF = upgate.shape[-1] // 2
    preact, upper = upgate[:, :FF], upgate[:, FF:]
    preact_sig = jax.nn.sigmoid(preact)
    swished = preact * preact_sig
    activated = (swished * upper).astype(bf16)
    trans = lax.optimization_barrier(mm(activated, reduce_full, (1,), (0,)))
    postgate_sig = jax.nn.sigmoid(postgate)
    mixed = (residual + postgate_sig * trans).astype(bf16)

    def owned(grad):
        return [g.reshape(G, T, g.shape[0] // W, D) for g in blocks(grad)]

    g_out = cotangent.reshape(S * R, D)
    trans_back = (postgate_sig * g_out).astype(bf16)
    postgate_back = g_out * trans * slope(postgate_sig)
    reducer_part = mm(activated, trans_back, (0,), (0,), bf16)
    act_back = mm(trans_back, reduce_full, (1,), (1,))
    up_back = jnp.concatenate(
        [act_back * upper * preact_sig * (1.0 + preact * (1.0 - preact_sig)), act_back * swished], axis=-1
    ).astype(bf16)
    expander_part = mm(posthidden, up_back, (0,), (0,), bf16)
    posthidden_back = mm(up_back, expand_full, (1,), (1,))
    postscale_back = posthidden_back * post_norm * slope(post_gain)
    residual_back = g_out + norm_back(post_norm, post_inv, posthidden_back * post_gain)
    branch_back = (pregate_sig * residual_back).astype(bf16)
    pregate_back = residual_back * branch * slope(pregate_sig)
    combiner_part = mm(gated, branch_back, (0,), (0,), bf16)
    gated_back = mm(branch_back, comb_full, (1,), (1,))
    gating_low = (attended * gated_back * slope(gating)).astype(bf16)
    gate_part = mm(pre, gating_low, (0,), (0,), bf16)
    second_part = jnp.concatenate(
        owned(expander_part) + owned(combiner_part) + owned(reducer_part) + owned(gate_part), axis=2
    )
    second_owned = pinned(second_part.reshape(G, -1, D))
    second_part = lax.psum_scatter(second_owned, "samp", scatter_dimension=0, tiled=False)

    attended_back = (gating * gated_back).astype(bf16)
    query_back, dkv, *bias_back = attention_back(
        me.astype(jnp.int32)[None], probs, attended_back.reshape(S, R, D), kv, query, second_owned, fold, G
    )
    query_back = query_back.reshape(S * R, D)
    dkv = dkv.reshape(S, 2 * D, N)

    later = jnp.concatenate([pregate_back, postscale_back, posthidden_back, postgate_back], axis=-1)
    later_sums = jnp.split(jnp.sum(later, axis=0), 4)
    later_low = later.astype(bf16)
    later_part = mm(later_low, cond_low, (0,), (0,), bf16)
    later_back = mm(later_low, cond_rest, (1,), (0,))

    pre_back_all = pinned(mm(dkv, proj_full[:, 2 * D :], (1,), (1,), bf16))
    if fold > 1:
        kept, given = bias_back
        bias_both = (kept.astype(f32) + hop(given, "samp", 1).astype(f32) + zero(pre_back_all).astype(f32)).astype(bf16)
        bias_sum = sum_samp_end(bias_both)
    else:
        bias_sum = sum_samp([bias_back[0].reshape(H * R, G, C).transpose(1, 0, 2)]).reshape(H, R, C)
    qg_low = jnp.concatenate([query_back.astype(bf16), gating_low], axis=-1)
    q_part = mm(pre, query_back.astype(bf16), (0,), (0,), bf16)
    kv_part = mm(pre_all.reshape(S, N, D), dkv, (0, 1), (0, 2), bf16)
    proj_owned = pinned(jnp.concatenate(owned(q_part) + owned(kv_part), axis=2).reshape(G, -1, D))
    proj_part = lax.psum_scatter(proj_owned, "samp", scatter_dimension=0, tiled=False)
    parts = sum_tok(pre_back_all.reshape(S, T, R, D), dim=1, apart=True)
    parts = [mm(qg_low, proj_full[:, : 2 * D], (1,), (1,))] + [p.reshape(S * R, D) for p in parts]
    tokens_grad, early_sums, early_part, singles_part, sample_sums = finish(
        parts, tokens_in.reshape(S * R, D), own(gain_all), residual_back, later_back, cond, cond_low, cond_pre,
        [proj_owned, bias_both if fold > 1 else bias_sum], S,
    )
    pair_grad, pairhead_part = pair_back(pairwise[0], bias_sum.transpose(1, 0, 2), pht, early_part, fold)
    offsets_part = jnp.concatenate([early_sums[0], later_sums[0], later_sums[1], later_sums[3]])
    shifts_part = jnp.concatenate([early_sums[1], later_sums[2]])
    querybias_part = jnp.sum(query_back, axis=0)
    cond_part = pinned(jnp.concatenate([early_part, later_part], axis=0).reshape(G, T * cc, CS))
    vec_part = jnp.concatenate(
        [offsets_part.reshape(G, T, no), shifts_part.reshape(G, T, ns), querybias_part.reshape(G, T, pr)], axis=-1
    )
    vec_part = jnp.zeros((G, T, 8, CS), bf16).at[:, :, 0, : vec.shape[0]].set(vec_part.astype(bf16))
    vec_part = pinned(vec_part.reshape(G, T * 8, CS))
    cs = CS // G
    extra = singles_part.reshape(G, cs, CS)
    extra = pinned(extra)
    cond_both = sum_samp_start([cond_part, vec_part, extra], bias_sum)
    second_part, proj_part = second_part.reshape(T, -1, D), proj_part.reshape(T, -1, D)
    both_part = jnp.concatenate([second_part + zero(cond_part).astype(bf16), proj_part], axis=1)
    both_sum = lax.psum_scatter(both_part, "tok", scatter_dimension=0, tiled=False).astype(f32)
    second_sum, proj_sum = both_sum[: second.shape[0]], both_sum[second.shape[0] :]
    both = sum_samp_end(cond_both)
    cond_half = jnp.concatenate([both[: T * cc].reshape(T, cc, CS), both[T * cc : T * (cc + 8)].reshape(T, 8, CS)], axis=1)
    singles_t = both[T * (cc + 8) :, :R]

    by_sample = jnp.concatenate(
        [sample_sums[:S], jnp.broadcast_to(jnp.where(t == 0, noise_level, 0)[:, None], (S, 128)).astype(f32)],
        axis=1,
    )
    placed = lax.dynamic_update_slice_in_dim(jnp.zeros((G * S, CS + 128), f32), by_sample, me * S, 0)
    small = everyone(jnp.concatenate([placed, jnp.pad(pairhead_part, ((0, 0), (0, CS)))], axis=0), cond_half)
    level_all = small[: G * S, CS].astype(jnp.int32)
    levels = jnp.arange(noise_table.shape[0], dtype=jnp.int32)
    level_hot = (levels[:, None] == level_all[None, :]).astype(f32)
    noise_grad = jnp.dot(level_hot, small[: G * S, :CS], precision=lax.Precision.HIGHEST)
    pairhead_grad = small[G * S :, : pairhead_part.shape[1]].T

    def unblocks(x, order):
        return jnp.concatenate([x[i * pr : (i + 1) * pr] for i in order], axis=1)

    cond_sum = sum_tok(cond_half.astype(bf16))
    cond_out, vec_out = cond_sum[:cc], cond_sum[cc]
    return (
        mixed.reshape(S, R, D),
        tokens_grad.reshape(S, R, D),
        singles_t.T[None],
        pair_grad[None],
        noise_grad,
        cond_out.T,
        vec_out[:no],
        vec_out[no : no + ns],
        unblocks(proj_sum, (1, 2, 3, 0)),
        vec_out[no + ns : no + ns + pr],
        second_sum[4 * pr : 5 * pr],
        unblocks(second_sum, (0, 1, 2, 3)),
        second_sum[5 * pr :],
        pairhead_grad,
    )


def solution(mesh):
    shard = ("samp", "tok")
    in_specs = (
        P("samp", "tok", None), P("samp", "tok", None), P(None, "tok", None), P(), P("samp"), P(),
        P(None, "tok", "samp", None), P(None, shard), P(shard), P(shard), P(shard, None), P(shard),
        P(shard, None), P(shard, None), P(shard, None), P(),
    )
    out_specs = (
        P("samp", "tok", None), P("samp", "tok", None), P(None, "tok", "samp"), P(None, "tok", "samp", None), P(),
        P(None, shard), P(shard), P(shard), P(shard, None), P(shard), P(shard, None), P(shard, None),
        P(shard, None), P(),
    )
    return jax.shard_map(per_device, mesh=mesh, in_specs=in_specs, out_specs=out_specs, check_vma=False)
```

```python
from jax.experimental.layout import Layout, with_layout_constraint
import jax
import jax.numpy as jnp
from jax import lax
from jax.experimental import pallas as pl
from jax.experimental.pallas import tpu as pltpu
from jax.sharding import PartitionSpec as P

DH = 48
EPS = 1e-5
WIN = 256
ROWS = 32
VMEM_BYTES = 56 * 1024 * 1024
f32 = jnp.float32
bf16 = jnp.bfloat16
COST = pl.CostEstimate(flops=1024, bytes_accessed=1024, transcendentals=0)
NT = (((1,), (1,)), ((), ()))
TN = (((0,), (0,)), ((), ()))


def params():
    return pltpu.CompilerParams(vmem_limit_bytes=VMEM_BYTES)


def window(h, width):
    w = pl.multiple_of(jnp.minimum((h * DH) // 128 * 128, width - WIN), 128)
    lane = lax.broadcasted_iota(jnp.int32, (1, WIN), 1) + w
    return w, (lane >= h * DH) & (lane < h * DH + DH)


def attention_body(q_ref, k_ref, v_ref, bias_ref, mask_ref, p_ref, att_ref, scores):
    samples, rows, width = q_ref.shape
    heads = bias_ref.shape[0]
    mask = mask_ref[...]
    windows = [window(pl.program_id(0) * heads + u, width) for u in range(heads)]
    for u, (w, inside) in enumerate(windows):
        for b in range(samples):
            q = jnp.where(inside, q_ref[b, :, pl.ds(w, WIN)], 0)
            scores[u * samples + b] = lax.dot_general(q, k_ref[b, :, pl.ds(w, WIN)], NT, preferred_element_type=f32)
    for u in range(heads):
        for i in range(0, rows, ROWS):
            bias = bias_ref[u, i : i + ROWS].astype(f32) + mask
            for b in range(samples):
                s = scores[u * samples + b, i : i + ROWS] * (DH ** -0.5) + bias
                e = jnp.exp(s - jnp.max(s, axis=1, keepdims=True))
                p_ref[u, b, i : i + ROWS] = (e * (1.0 / jnp.sum(e, axis=1, keepdims=True))).astype(bf16)
    for u, (w, inside) in enumerate(windows):
        for b in range(samples):
            o = jnp.dot(p_ref[u, b], v_ref[b, :, pl.ds(w, WIN)], preferred_element_type=f32)
            att_ref[b, :, pl.ds(w, WIN)] = jnp.where(inside, o, att_ref[b, :, pl.ds(w, WIN)])


def attention(q, kv, bias, mask):
    S, R, D = q.shape
    N, H = kv.shape[1], bias.shape[0]
    heads = 4

    def whole(*shape):
        return pl.BlockSpec(shape, lambda h: (0,) * len(shape))

    return pl.pallas_call(
        attention_body,
        grid=(H // heads,),
        in_specs=[
            whole(S, R, D),
            whole(S, N, D),
            pl.BlockSpec((S, N, D), lambda h: (0, 0, 1)),
            pl.BlockSpec((heads, R, N), lambda h: (h, 0, 0)),
            whole(1, N),
        ],
        out_specs=[pl.BlockSpec((heads, S, R, N), lambda h: (h, 0, 0, 0)), whole(S, R, D)],
        out_shape=[jax.ShapeDtypeStruct((H, S, R, N), bf16), jax.ShapeDtypeStruct((S, R, D), f32)],
        scratch_shapes=[pltpu.VMEM((heads * S, R, N), f32)],
        compiler_params=params(),
        cost_estimate=COST,
        name="attention",
    )(q, kv, kv, bias, mask)


def attention_back_body(fold, me_ref, p_ref, do_ref, k_ref, v_ref, q_ref, dq_ref, dkv_ref, *rest):
    *bb_refs, qt, dot_, dp_all, low_all, acc = rest
    samples, rows, width = do_ref.shape
    heads = p_ref.shape[0]
    step = pl.program_id(0)

    @pl.when(step == 0)
    def _():
        for b in range(samples):
            qt[b] = q_ref[b].astype(f32).T.astype(bf16)
            dot_[b] = do_ref[b].astype(f32).T.astype(bf16)

    windows = [window(step * heads + u, width) for u in range(heads)]
    for u, (w, inside) in enumerate(windows):
        for b in range(samples):
            do = jnp.where(inside, do_ref[b, :, pl.ds(w, WIN)], 0)
            dp_all[u * samples + b] = lax.dot_general(do, v_ref[b, :, pl.ds(w, WIN)], NT, preferred_element_type=f32)
    for u in range(heads):
        for i in range(0, rows, ROWS):
            total = None
            for b in range(samples):
                dp = dp_all[u * samples + b, i : i + ROWS]
                p = p_ref[u, b, i : i + ROWS].astype(f32)
                ds = p * (dp - jnp.sum(p * dp, axis=1, keepdims=True))
                low_all[u * samples + b, i : i + ROWS] = ds.astype(bf16)
                total = ds if total is None else total + ds
            acc[u, i : i + ROWS] = total
    for u, (w, inside) in enumerate(windows):
        own = pl.ds(pl.multiple_of((step * heads + u) * DH, 16), DH)
        for b in range(samples):
            low = low_all[u * samples + b]
            dq = jnp.dot(low, k_ref[b, :, pl.ds(w, WIN)], preferred_element_type=f32) * (DH ** -0.5)
            dq_ref[b, :, pl.ds(w, WIN)] = jnp.where(inside, dq, dq_ref[b, :, pl.ds(w, WIN)])
            dk = jnp.dot(qt[b, own, :], low, preferred_element_type=f32) * (DH ** -0.5)
            dv = jnp.dot(dot_[b, own, :], p_ref[u, b], preferred_element_type=f32)
            dkv_ref[b, 0, u * DH : (u + 1) * DH] = dk.astype(bf16)
            dkv_ref[b, 1, u * DH : (u + 1) * DH] = dv.astype(bf16)
        if fold == 1:
            bb_refs[0][u] = acc[u].astype(bf16)
            continue
        kept_ref, given_ref = bb_refs
        count, _, part, lanes = kept_ref.shape
        c = lanes // fold
        odd = me_ref[0] % 2 == 1

        def piece(s):
            return jnp.concatenate(
                [acc[u, i * part : (i + 1) * part, s * c : (s + 1) * c] for i in range(fold)], axis=1
            )

        for j in range(count):
            first, second = piece(2 * j), piece(2 * j + 1)
            kept_ref[j, u] = jnp.where(odd, second, first).astype(bf16)
            given_ref[j, u] = jnp.where(odd, first, second).astype(bf16)


def attention_back(me, p, do, kv, q, first, fold, groups):
    H, S, R, N = p.shape
    D = do.shape[2]
    heads = 2

    def whole(*shape):
        return pl.BlockSpec(shape, lambda h, m: (0,) * len(shape))

    if fold == 1:
        bb_specs, bb_shapes = [pl.BlockSpec((heads, R, N), lambda h, m: (h, 0, 0))], [(H, R, N)]
    else:
        tail = (R // fold, fold * (N // groups))
        bb_specs = [pl.BlockSpec((groups // 2, heads) + tail, lambda h, m: (0, h, 0, 0))] * 2
        bb_shapes = [(groups // 2, H) + tail] * 2

    def body(me_ref, p_ref, do_ref, k_ref, v_ref, q_ref, _, *refs):
        attention_back_body(fold, me_ref, p_ref, do_ref, k_ref, v_ref, q_ref, *refs)

    return pl.pallas_call(
        body,
        grid_spec=pltpu.PrefetchScalarGridSpec(
            num_scalar_prefetch=1,
            grid=(H // heads,),
            in_specs=[
                pl.BlockSpec((heads, S, R, N), lambda h, m: (h, 0, 0, 0)),
                whole(S, R, D),
                whole(S, N, D),
                pl.BlockSpec((S, N, D), lambda h, m: (0, 0, 1)),
                whole(S, R, D),
                pl.BlockSpec(memory_space=pl.ANY),
            ],
            out_specs=[whole(S, R, D), pl.BlockSpec((S, 2, heads * DH, N), lambda h, m: (0, 0, h, 0))] + bb_specs,
            scratch_shapes=[
                pltpu.VMEM((S, D, R), bf16),
                pltpu.VMEM((S, D, R), bf16),
                pltpu.VMEM((heads * S, R, N), f32),
                pltpu.VMEM((heads * S, R, N), bf16),
                pltpu.VMEM((heads, R, N), f32),
            ],
        ),
        out_shape=[
            jax.ShapeDtypeStruct((S, R, D), f32),
            jax.ShapeDtypeStruct((S, 2, D, N), bf16),
        ]
        + [jax.ShapeDtypeStruct(shape, bf16) for shape in bb_shapes],
        compiler_params=params(),
        cost_estimate=COST,
        name="attention_back",
    )(me, p, do, kv, kv, q, first)


def normal_rows(x):
    c = x - jnp.mean(x, axis=-1, keepdims=True)
    r = lax.rsqrt(jnp.mean(c * c, axis=-1, keepdims=True) + EPS)
    return c * r, r


def split(x):
    hi = x.astype(bf16)
    return hi, (x - hi.astype(f32)).astype(bf16)


def lane_mean(x):
    ones = jnp.full((x.shape[1], x.shape[1]), 1.0, bf16)
    hi, lo = split(x)
    total = jnp.dot(hi, ones, preferred_element_type=f32) + jnp.dot(lo, ones, preferred_element_type=f32)
    return total * (1.0 / x.shape[1])


def pair_bias_body(x_ref, ph_ref, out_ref, buf):
    fold, n, C, E = x_ref.shape
    ph = ph_ref[...]
    for i in range(n):
        x = x_ref[:, i].reshape(fold * C, E) if fold > 1 else x_ref[0, i]
        nrm, _ = normal_rows(x.astype(f32))
        buf[:, i, :] = lax.dot_general(ph, nrm.astype(bf16), NT, preferred_element_type=f32)
    out_ref[...] = buf[...].astype(bf16)


def pair_bias(x, pht, fold):
    R, C, E = x.shape
    H = pht.shape[0]
    rows = R // fold
    blk = 16
    return pl.pallas_call(
        pair_bias_body,
        grid=(rows // blk,),
        in_specs=[
            pl.BlockSpec((fold, blk, C, E), lambda i: (0, i, 0, 0)), pl.BlockSpec((H, E), lambda i: (0, 0)),
        ],
        out_specs=pl.BlockSpec((H, blk, fold * C), lambda i: (0, i, 0)),
        out_shape=jax.ShapeDtypeStruct((H, rows, fold * C), bf16),
        scratch_shapes=[pltpu.VMEM((H, blk, fold * C), f32)],
        compiler_params=params(),
        cost_estimate=COST,
        name="pair_bias",
    )(x.reshape(fold, rows, C, E), pht)


def pair_back_body(x_ref, bb_ref, ph_ref, _, out_ref, dph_ref):
    fold, n, C, E = x_ref.shape
    H = ph_ref.shape[0]
    ph = ph_ref[...].astype(f32)
    ph_hi, ph_lo = split(ph - jnp.mean(ph, axis=-1, keepdims=True))
    ph4 = jnp.concatenate([ph_hi, ph_lo, ph_hi, ph_lo], axis=0)
    acc = jnp.zeros((2 * H, E), f32)
    for i in range(n):
        x = x_ref[:, i].reshape(fold * C, E) if fold > 1 else x_ref[0, i]
        nrm, r = normal_rows(x.astype(f32))
        hi, lo = split(bb_ref[i])
        g = lax.dot_general(
            jnp.concatenate([hi, hi, lo, lo], axis=0), ph4, TN, preferred_element_type=f32
        )
        grad = r * (g - nrm * lane_mean(g * nrm))
        if fold > 1:
            out_ref[:, i] = grad.reshape(fold, C, E)
        else:
            out_ref[0, i] = grad
        acc += jnp.dot(jnp.concatenate([hi, lo], axis=0), nrm.astype(bf16), preferred_element_type=f32)
    part = acc[:H] + acc[H:]

    @pl.when(pl.program_id(0) == 0)
    def _():
        dph_ref[...] = part

    @pl.when(pl.program_id(0) != 0)
    def _():
        dph_ref[...] += part


def pair_back(x, bb, pht, first, fold):
    R, C, E = x.shape
    H = pht.shape[0]
    rows = R // fold
    blk = 8
    grad, dph = pl.pallas_call(
        pair_back_body,
        grid=(rows // blk,),
        in_specs=[
            pl.BlockSpec((fold, blk, C, E), lambda i: (0, i, 0, 0)),
            pl.BlockSpec((blk, H, fold * C), lambda i: (i, 0, 0)),
            pl.BlockSpec((H, E), lambda i: (0, 0)),
            pl.BlockSpec(memory_space=pl.ANY),
        ],
        out_specs=[pl.BlockSpec((fold, blk, C, E), lambda i: (0, i, 0, 0)), pl.BlockSpec((H, E), lambda i: (0, 0))],
        out_shape=[jax.ShapeDtypeStruct((fold, rows, C, E), f32), jax.ShapeDtypeStruct((H, E), f32)],
        compiler_params=params(),
        cost_estimate=COST,
        name="pair_back",
    )(x.reshape(fold, rows, C, E), bb, pht, first)
    return grad.reshape(R, C, E), dph


def lay_bias_body(me_ref, *refs):
    pieces, (out_ref, slots, sems) = refs[:-3], refs[-3:]
    h = pl.program_id(0)
    part, lanes = slots.shape[2:]
    fold = out_ref.shape[1] // part
    c = lanes // fold

    @pl.when(h == 0)
    def _():
        copies = [
            pltpu.make_async_copy(p, slots.at[jnp.bitwise_xor(me_ref[0], k)], sems.at[k]) for k, p in enumerate(pieces)
        ]
        for copy in copies:
            copy.start()
        for copy in copies:
            copy.wait()

    laid = [slots[s, h].astype(f32) for s in range(len(pieces))]
    for i in range(fold):
        out_ref[0, i * part : (i + 1) * part, :] = jnp.concatenate(
            [p[:, i * c : (i + 1) * c] for p in laid], axis=1
        ).astype(bf16)


def lay_bias(me, pieces, rows):
    H, part, lanes = pieces[0].shape
    count = len(pieces)
    keys = count * lanes // (rows // part)
    return pl.pallas_call(
        lay_bias_body,
        grid_spec=pltpu.PrefetchScalarGridSpec(
            num_scalar_prefetch=1,
            grid=(H,),
            in_specs=[pl.BlockSpec(memory_space=pl.ANY)] * count,
            out_specs=pl.BlockSpec((1, rows, keys), lambda h, s: (h, 0, 0)),
            scratch_shapes=[pltpu.VMEM((count, H, part, lanes), bf16), pltpu.SemaphoreType.DMA((count,))],
        ),
        out_shape=jax.ShapeDtypeStruct((H, rows, keys), bf16),
        compiler_params=params(),
        cost_estimate=COST,
        name="lay_bias",
    )(me, *pieces)


def lay_vectors_body(counts, x_ref, out_ref):
    x = x_ref[...]
    D = out_ref.shape[1]
    row = start = 0
    for n in counts:
        per = D // n
        for i in range(x.shape[0] // per):
            pieces = [x[j : j + 1, start : start + n] for j in range(i * per, (i + 1) * per)]
            out_ref[row : row + 1, :] = jnp.concatenate(pieces, axis=1)
            row += 1
        start += n
    out_ref[row:, :] = jnp.zeros((out_ref.shape[0] - row, D), f32)


def lay_vectors(x, *counts):
    D = x.shape[1]

    def body(x_ref, out_ref):
        lay_vectors_body(counts, x_ref, out_ref)

    return pl.pallas_call(
        body,
        out_shape=jax.ShapeDtypeStruct((8, D), f32),
        compiler_params=params(),
        cost_estimate=COST,
        name="lay_vectors",
    )(x)


def center(n, r, g):
    return r * (g - jnp.mean(g, axis=-1, keepdims=True) - n * jnp.mean(g * n, axis=-1, keepdims=True))


def finish(parts, tokens, scale_row, residual_back, later_back, cond, cond_low, cond_pre, first, samples):
    rows, D = tokens.shape
    CS = cond.shape[1]
    count = len(parts)

    def body(*refs):
        x = refs[0][...].astype(f32)
        for p in refs[1:count]:
            x = x + p[...].astype(f32)
        tok, gain_ref, resid, later, cond_ref, low_ref, pre_ref = refs[count : count + 7]
        grad, sums, part, single, by_sample = refs[count + 7 + len(first) :]
        n, r = normal_rows(tok[...].astype(f32))
        g = lax.dot_general(low_ref[...], pre_ref[:D], NT, preferred_element_type=f32)
        g = jax.nn.sigmoid(g + gain_ref[...])
        scale = x * n * (g * (1.0 - g))
        grad[...] = resid[...] + center(n, r, x * g)
        sums[...] = jnp.zeros_like(sums)
        sums[0:1, :] = jnp.sum(scale, axis=0, keepdims=True)
        sums[1:2, :] = jnp.sum(x, axis=0, keepdims=True)
        early = jnp.concatenate([scale.astype(bf16), x.astype(bf16)], axis=1)
        part[...] = lax.dot_general(early, low_ref[...], TN, preferred_element_type=f32).astype(bf16)
        back = later[...] + jnp.dot(early, pre_ref[...], preferred_element_type=f32)
        cond_grad = center(*normal_rows(cond_ref[...]), back)
        each = rows // samples
        total = cond_grad[:each]
        for b in range(1, samples):
            total = total + cond_grad[b * each : (b + 1) * each]
        single[...] = jnp.concatenate([total.T, jnp.zeros((CS, CS - each), f32)], axis=1).astype(bf16)
        by_sample[...] = jnp.zeros_like(by_sample)
        for b in range(samples):
            by_sample[b : b + 1, :] = jnp.sum(cond_grad[b * each : (b + 1) * each], axis=0, keepdims=True)

    shapes = [(rows, D), (8, D), (2 * D, CS), (CS, CS), (8, CS)]
    kinds = [f32, f32, bf16, bf16, f32]
    vmem = pl.BlockSpec(memory_space=pltpu.VMEM)
    return pl.pallas_call(
        body,
        in_specs=[vmem] * (count + 7) + [pl.BlockSpec(memory_space=pl.ANY)] * len(first),
        out_specs=[vmem] * 5,
        out_shape=[jax.ShapeDtypeStruct(s, kind) for s, kind in zip(shapes, kinds)],
        compiler_params=params(),
        cost_estimate=COST,
        name="finish",
    )(*parts, tokens, scale_row, residual_back, later_back, cond, cond_low, cond_pre, *first)


def prepare_body(tok_ref, single_ref, noise_ref, cond_ref, scale_ref, shift_ref, w_ref, pre_ref, kv_ref):
    D = tok_ref.shape[2]
    low = normal_rows(single_ref[...].astype(f32) + noise_ref[0])[0].astype(bf16)
    tok = normal_rows(tok_ref[0].astype(f32))[0]
    scale = lax.dot_general(low, cond_ref[:D], NT, preferred_element_type=f32) + scale_ref[...]
    shift = lax.dot_general(low, cond_ref[D:], NT, preferred_element_type=f32) + shift_ref[...]
    pre = (jax.nn.sigmoid(scale) * tok + shift).astype(bf16)
    pre_ref[0] = pre
    kv_ref[0] = jnp.dot(pre, w_ref[...], preferred_element_type=f32).astype(bf16)


def prepare(tokens, singles, noise, cond_pre, scale_row, shift_row, projector):
    S, N, D = tokens.shape
    CS = singles.shape[1]

    def whole(*shape):
        return pl.BlockSpec(shape, lambda b: (0,) * len(shape))

    def each(*shape):
        return pl.BlockSpec((1,) + shape, lambda b: (b,) + (0,) * len(shape))

    return pl.pallas_call(
        prepare_body,
        grid=(S,),
        in_specs=[
            each(N, D), whole(N, CS), each(1, CS), whole(2 * D, CS), whole(1, D), whole(1, D),
            pl.BlockSpec((D, 2 * D), lambda b: (0, 1)),
        ],
        out_specs=[each(N, D), each(N, 2 * D)],
        out_shape=[jax.ShapeDtypeStruct((S, N, D), bf16), jax.ShapeDtypeStruct((S, N, 2 * D), bf16)],
        compiler_params=params(),
        cost_estimate=COST,
        name="prepare",
    )(tokens, singles, noise[:, None], cond_pre, scale_row, shift_row, projector)


def pinned(x):
    return with_layout_constraint(x, Layout(major_to_minor=tuple(range(x.ndim))))


def norm_back(n, r, g):
    return r * (g - jnp.mean(g, axis=-1, keepdims=True) - n * jnp.mean(g * n, axis=-1, keepdims=True))


def slope(s):
    return s * (1.0 - s)


def mm(a, b, ca, cb, out=f32):
    return lax.dot_general(a, b, ((ca, cb), ((), ())), preferred_element_type=f32).astype(out)


def hop(x, axis, k):
    return lax.ppermute(x, axis, [(i, i ^ k) for i in range(lax.axis_size(axis))])


def at(x, i):
    return lax.dynamic_index_in_dim(x, i, 0, keepdims=False)


def everyone(x, *others):
    steps = [(axis, 1 << i) for axis in ("tok", "samp") for i in range((lax.axis_size(axis) - 1).bit_length())]
    for i, (axis, k) in enumerate(steps):
        x = x + hop(x, axis, k)
        if i == 0:
            x = x + zero(*others).astype(f32)
    return x


def zero(*others):
    corners = [lax.slice(o, (0,) * o.ndim, (1,) * o.ndim).reshape(()).astype(f32) for o in others]
    return sum((jnp.abs(c) > 1e30).astype(jnp.int32) for c in corners)


def gather_tok(parts, others):
    n, t = lax.axis_size("tok"), lax.axis_index("tok")
    width = parts[0][0].shape[-1]
    rows = [p.size // width for p, _ in parts]
    x = jnp.concatenate([p.reshape(-1, width) for p, _ in parts], axis=0)
    up, down = [x], [x]
    for _ in range(1, n):
        up.append(lax.ppermute(up[-1], "tok", [(i, i + 1) for i in range(n - 1)]))
        down.append(lax.ppermute(down[-1], "tok", [(i + 1, i) for i in range(n - 1)]))
    outs, start = [], 0
    for i, ((p, dim), count) in enumerate(zip(parts, rows)):
        place = t + n + zero(*others[i])
        out = jnp.zeros(p.shape[:dim] + (n,) + p.shape[dim:], p.dtype)
        for k in range(n):
            got = [u[start : start + count].reshape(p.shape) for u in (up[k], down[n - k if k else 0])]
            got = got[0] if k == 0 else jnp.where(t >= k, *got)
            out = lax.dynamic_update_slice_in_dim(out, jnp.expand_dims(got, dim), (place - k) % n, dim)
        outs.append(out)
        start += count
    return outs


def sum_tok(x, *others, dim=0, apart=False):
    n, t = lax.axis_size("tok"), lax.axis_index("tok")
    x = x.reshape(x.shape[:dim] + (n // 2, 2) + x.shape[dim + 1 :])

    def part(v, i, d):
        return lax.dynamic_index_in_dim(v, i, d, keepdims=False)

    came = hop(part(x, 1 - t % 2, dim + 1), "tok", 1)
    pair = part(x, t % 2, dim + 1).astype(f32) + came.astype(f32)
    given = [hop(part(pair, (t // 2) ^ k, dim).astype(bf16), "tok", 2 * k) for k in range(1, n // 2)]
    total = part(pair, t // 2 + (zero(*others) if others else 0), dim)
    if apart:
        return [total] + given
    for g in given:
        total = total + g.astype(f32)
    return total


def sum_samp_start(parts, *others):
    n = lax.axis_size("samp")
    if n != 8:
        return jnp.concatenate([p.astype(bf16) for p in parts], axis=-2)
    c = lax.axis_index("samp") % 2

    def half(which):
        picked = [
            lax.dynamic_index_in_dim(p.reshape((n // 2, 2) + p.shape[1:]), which, 1, keepdims=False) for p in parts
        ]
        return jnp.concatenate(picked, axis=-2) if len(picked) > 1 else picked[0]

    other = hop(half(1 - c).astype(bf16), "samp", 1)
    both = half(c + zero(*others)).astype(f32) + other.astype(f32)
    return pinned(both.astype(bf16))


def sum_samp_end(both):
    n = lax.axis_size("samp")
    if n != 8:
        return lax.psum_scatter(both, "samp", scatter_dimension=0, tiled=False).astype(f32)
    j = lax.axis_index("samp") // 2
    total = at(both, j).astype(f32)
    for k in range(1, n // 2):
        total = total + hop(at(both, j ^ k), "samp", 2 * k).astype(f32)
    return total


def sum_samp(parts):
    return sum_samp_end(sum_samp_start(parts))


def per_device(
    tokens_in, cotangent, singles, noise_table, noise_level, pad_mask, pairwise, conditioner,
    offsets, shifts, projector, querybias, combiner, expander, reducer, pairhead,
):
    S, R, D = tokens_in.shape
    C = pairwise.shape[2]
    N = pad_mask.shape[1]
    H = pairhead.shape[1]
    CS = conditioner.shape[0]
    T, G = lax.axis_size("tok"), lax.axis_size("samp")
    W = G * T
    t, me = lax.axis_index("tok"), lax.axis_index("samp")
    fold = 4 if G == 8 else 1

    def blocks(w):
        return [w[:, i * D : (i + 1) * D] for i in range(w.shape[1] // D)]

    def rows_of(buf, start, count):
        return buf[:, start : start + count].reshape(W * count, D)

    cond_t = conditioner.T
    cc, pr, rr = cond_t.shape[0], projector.shape[0], reducer.shape[0]
    no, ns = offsets.shape[0], shifts.shape[0]
    vec = jnp.concatenate([offsets, shifts, querybias])
    vec_row = jnp.zeros((8, D), bf16).at[0, : vec.shape[0]].set(vec)
    cond_rows = jnp.concatenate([cond_t[: cc // 2], cond_t[cc // 2 :]], axis=1)
    q_block, k_block, v_block, g_block = blocks(projector)
    mine = lax.dynamic_slice_in_dim(singles[0], me * (R // G), R // G, 0)
    if R % (2 * G) == 0:
        single = jnp.concatenate([mine[: R // G // 2], mine[R // G // 2 :]], axis=1)
    else:
        single = jnp.pad(mine, ((0, 0), (0, D - CS)))
    single_rows = single.shape[0]
    first = jnp.concatenate([q_block, g_block, k_block, v_block, cond_rows, vec_row, single], axis=0)
    second = jnp.concatenate(blocks(expander) + [combiner, reducer], axis=0)
    first_all = lax.all_gather(first, ("samp", "tok"), axis=0)

    pht = pairhead.T
    piece = pair_bias(pairwise[0], pht, fold)
    if fold > 1:
        even = [piece] + [hop(piece, "samp", k) for k in range(2, G, 2)]
        pieces = [p for e in even for p in (e, hop(e, "samp", 1))]
        bias_all = lay_bias(me.astype(jnp.int32)[None], pieces, R)
    else:
        bias_all = jnp.transpose(lax.all_gather(piece, "samp", axis=0), (1, 2, 0, 3)).reshape(H, R, N)
    mask_add = (pad_mask.astype(f32) - 1.0) * 1e9
    ready = lax.dynamic_index_in_dim(first_all, zero(bias_all), 0)
    tokens_all, second_mine = gather_tok([(tokens_in, 1), (second, 0)], [[bias_all], [ready]])
    second_all = lax.all_gather(second_mine, "samp", axis=0).reshape(W, second.shape[0], D)

    tokens_all = tokens_all.reshape(S * N, D)
    singles_all = first_all[:, -single_rows:].reshape(G, T, single_rows, D).transpose(1, 0, 2, 3)
    if single_rows * 2 == R // G:
        halves = [singles_all[:, :, :, :CS], singles_all[:, :, :, CS:]]
        singles_all = jnp.concatenate(halves, axis=2).reshape(N, CS)
    else:
        singles_all = singles_all[:, :, :, :CS].reshape(N, CS)
    levels = jnp.arange(noise_table.shape[0], dtype=jnp.int32)
    noise_rows = jnp.dot(
        (noise_level[:, None] == levels[None, :]).astype(f32), noise_table, precision=lax.Precision.HIGHEST
    )
    cond = (singles.astype(f32) + noise_rows[:, None]).reshape(S * R, CS)
    cond_low = normal_rows(cond)[0].astype(bf16)
    tokens = tokens_in.reshape(S * R, D).astype(f32)

    def own(x):
        return lax.dynamic_slice_in_dim(x.reshape(S, N, x.shape[-1]), t * R, R, 1).reshape(S * R, x.shape[-1])

    proj_full = jnp.concatenate([rows_of(first_all, i * pr, pr) for i in range(4)], axis=1)
    def cond_rows_of(start, stop):
        a, b = start // cc, -(-stop // cc)
        part = first_all[a:b, 4 * pr : 4 * pr + cc // 2]
        part = jnp.concatenate([part[:, :, :CS], part[:, :, CS:]], axis=1).reshape((b - a) * cc, CS)
        return part[start - a * cc : stop - a * cc]

    cond_pre, cond_rest = cond_rows_of(0, 2 * D), cond_rows_of(2 * D, 6 * D)
    vecs = first_all[:, 4 * pr + cc // 2].astype(f32)
    if fold > 1:
        rows = lay_vectors(vecs, no, ns, pr)
        o, sh, querybias_full = [rows[i : i + 1] for i in range(4)], [rows[4:5], rows[5:6]], rows[6:7]
    else:
        o = jnp.split(vecs[:, :no].reshape(1, W * no), 4, axis=1)
        sh = jnp.split(vecs[:, no : no + ns].reshape(1, W * ns), 2, axis=1)
        querybias_full = vecs[:, no + ns : no + ns + pr].reshape(1, W * pr)

    pre_all, kv = prepare(
        tokens_all.reshape(S, N, D), singles_all, noise_rows, cond_pre, o[0], sh[0], proj_full
    )
    pre = own(pre_all)
    query = (mm(pre, proj_full[:, :D], (1,), (0,)) + querybias_full).astype(bf16).reshape(S, R, D)
    gating = jax.nn.sigmoid(mm(pre, proj_full[:, D : 2 * D], (1,), (0,)))

    probs, attended = attention(query, kv, bias_all, mask_add)
    attended = attended.reshape(S * R, D)

    adapt_own = mm(cond_low, cond_rest, (1,), (1,)) + jnp.concatenate([o[1], o[2], sh[1], o[3]], axis=1)
    pregate, postscale, postshift, postgate = jnp.split(adapt_own, 4, axis=-1)
    expand_full = pinned(jnp.concatenate([rows_of(second_all, i * pr, pr) for i in range(4)], axis=1))
    comb_full = rows_of(second_all, 4 * pr, pr)
    reduce_full = rows_of(second_all, 5 * pr, rr)

    gated = (gating * attended).astype(bf16)
    branch = mm(gated, comb_full, (1,), (0,))
    pregate_sig = jax.nn.sigmoid(pregate)
    residual = tokens + pregate_sig * branch
    post_norm, post_inv = normal_rows(residual)
    post_gain = jax.nn.sigmoid(postscale)
    posthidden = (post_gain * post_norm + postshift).astype(bf16)
    upgate = mm(posthidden, expand_full, (1,), (0,))
    FF = upgate.shape[-1] // 2
    preact, upper = upgate[:, :FF], upgate[:, FF:]
    preact_sig = jax.nn.sigmoid(preact)
    swished = preact * preact_sig
    activated = (swished * upper).astype(bf16)
    trans = lax.optimization_barrier(mm(activated, reduce_full, (1,), (0,)))
    postgate_sig = jax.nn.sigmoid(postgate)
    mixed = (residual + postgate_sig * trans).astype(bf16)

    def owned(grad):
        return [g.reshape(G, T, g.shape[0] // W, D) for g in blocks(grad)]

    g_out = cotangent.reshape(S * R, D)
    trans_back = (postgate_sig * g_out).astype(bf16)
    postgate_back = g_out * trans * slope(postgate_sig)
    reducer_part = mm(activated, trans_back, (0,), (0,), bf16)
    act_back = mm(trans_back, reduce_full, (1,), (1,))
    up_back = jnp.concatenate(
        [act_back * upper * preact_sig * (1.0 + preact * (1.0 - preact_sig)), act_back * swished], axis=-1
    ).astype(bf16)
    expander_part = mm(posthidden, up_back, (0,), (0,), bf16)
    posthidden_back = mm(up_back, expand_full, (1,), (1,))
    postscale_back = posthidden_back * post_norm * slope(post_gain)
    residual_back = g_out + norm_back(post_norm, post_inv, posthidden_back * post_gain)
    branch_back = (pregate_sig * residual_back).astype(bf16)
    pregate_back = residual_back * branch * slope(pregate_sig)
    combiner_part = mm(gated, branch_back, (0,), (0,), bf16)
    gated_back = mm(branch_back, comb_full, (1,), (1,))
    gating_low = (attended * gated_back * slope(gating)).astype(bf16)
    gate_part = mm(pre, gating_low, (0,), (0,), bf16)
    second_part = jnp.concatenate(
        owned(expander_part) + owned(combiner_part) + owned(reducer_part) + owned(gate_part), axis=2
    )
    second_owned = pinned(second_part.reshape(G, -1, D))
    second_part = lax.psum_scatter(second_owned, "samp", scatter_dimension=0, tiled=False)

    attended_back = (gating * gated_back).astype(bf16)
    query_back, dkv, *bias_back = attention_back(
        me.astype(jnp.int32)[None], probs, attended_back.reshape(S, R, D), kv, query, second_owned, fold, G
    )
    query_back = query_back.reshape(S * R, D)
    dkv = dkv.reshape(S, 2 * D, N)

    later = jnp.concatenate([pregate_back, postscale_back, posthidden_back, postgate_back], axis=-1)
    later_sums = jnp.split(jnp.sum(later, axis=0), 4)
    later_low = later.astype(bf16)
    later_part = mm(later_low, cond_low, (0,), (0,), bf16)
    later_back = mm(later_low, cond_rest, (1,), (0,))

    pre_back_all = pinned(mm(dkv, proj_full[:, 2 * D :], (1,), (1,), bf16))
    if fold > 1:
        kept, given = bias_back
        bias_both = (kept.astype(f32) + hop(given, "samp", 1).astype(f32) + zero(pre_back_all).astype(f32)).astype(bf16)
        bias_sum = sum_samp_end(bias_both)
    else:
        bias_sum = sum_samp([bias_back[0].reshape(H * R, G, C).transpose(1, 0, 2)]).reshape(H, R, C)
    qg_low = jnp.concatenate([query_back.astype(bf16), gating_low], axis=-1)
    q_part = mm(pre, query_back.astype(bf16), (0,), (0,), bf16)
    kv_part = mm(pre_all.reshape(S, N, D), dkv, (0, 1), (0, 2), bf16)
    proj_owned = pinned(jnp.concatenate(owned(q_part) + owned(kv_part), axis=2).reshape(G, -1, D))
    proj_part = lax.psum_scatter(proj_owned, "samp", scatter_dimension=0, tiled=False)
    parts = sum_tok(pre_back_all.reshape(S, T, R, D), dim=1, apart=True)
    parts = [mm(qg_low, proj_full[:, : 2 * D], (1,), (1,))] + [p.reshape(S * R, D) for p in parts]
    tokens_grad, early_sums, early_part, singles_part, sample_sums = finish(
        parts, tokens_in.reshape(S * R, D), o[0], residual_back, later_back, cond, cond_low, cond_pre,
        [proj_owned, bias_both if fold > 1 else bias_sum], S,
    )
    pair_grad, pairhead_part = pair_back(pairwise[0], bias_sum.transpose(1, 0, 2), pht, early_part, fold)
    offsets_part = jnp.concatenate([early_sums[0], later_sums[0], later_sums[1], later_sums[3]])
    shifts_part = jnp.concatenate([early_sums[1], later_sums[2]])
    querybias_part = jnp.sum(query_back, axis=0)
    cond_part = pinned(jnp.concatenate([early_part, later_part], axis=0).reshape(G, T * cc, CS))
    vec_part = jnp.concatenate(
        [offsets_part.reshape(G, T, no), shifts_part.reshape(G, T, ns), querybias_part.reshape(G, T, pr)], axis=-1
    )
    vec_part = jnp.zeros((G, T, 8, CS), bf16).at[:, :, 0, : vec.shape[0]].set(vec_part.astype(bf16))
    vec_part = pinned(vec_part.reshape(G, T * 8, CS))
    cs = CS // G
    extra = singles_part.reshape(G, cs, CS)
    extra = pinned(extra)
    cond_both = sum_samp_start([cond_part, vec_part, extra], bias_sum)
    second_part, proj_part = second_part.reshape(T, -1, D), proj_part.reshape(T, -1, D)
    both_part = jnp.concatenate([second_part + zero(pairhead_part).astype(bf16), proj_part], axis=1)
    both_sum = lax.psum_scatter(both_part, "tok", scatter_dimension=0, tiled=False).astype(f32)
    second_sum, proj_sum = both_sum[: second.shape[0]], both_sum[second.shape[0] :]
    both = sum_samp_end(cond_both)
    cond_half = jnp.concatenate([both[: T * cc].reshape(T, cc, CS), both[T * cc : T * (cc + 8)].reshape(T, 8, CS)], axis=1)
    singles_t = both[T * (cc + 8) :, :R]

    by_sample = jnp.concatenate(
        [sample_sums[:S], jnp.broadcast_to(jnp.where(t == 0, noise_level, 0)[:, None], (S, 128)).astype(f32)],
        axis=1,
    )
    placed = lax.dynamic_update_slice_in_dim(jnp.zeros((G * S, CS + 128), f32), by_sample, me * S, 0)
    small = everyone(jnp.concatenate([placed, jnp.pad(pairhead_part, ((0, 0), (0, CS)))], axis=0), cond_half)
    level_all = small[: G * S, CS].astype(jnp.int32)
    levels = jnp.arange(noise_table.shape[0], dtype=jnp.int32)
    level_hot = (levels[:, None] == level_all[None, :]).astype(f32)
    noise_grad = jnp.dot(level_hot, small[: G * S, :CS], precision=lax.Precision.HIGHEST)
    pairhead_grad = small[G * S :, : pairhead_part.shape[1]].T

    def unblocks(x, order):
        return jnp.concatenate([x[i * pr : (i + 1) * pr] for i in order], axis=1)

    cond_sum = sum_tok(cond_half.astype(bf16))
    cond_out, vec_out = cond_sum[:cc], cond_sum[cc]
    return (
        mixed.reshape(S, R, D),
        tokens_grad.reshape(S, R, D),
        singles_t.T[None],
        pair_grad[None],
        noise_grad,
        cond_out.T,
        vec_out[:no],
        vec_out[no : no + ns],
        unblocks(proj_sum, (1, 2, 3, 0)),
        vec_out[no + ns : no + ns + pr],
        second_sum[4 * pr : 5 * pr],
        unblocks(second_sum, (0, 1, 2, 3)),
        second_sum[5 * pr :],
        pairhead_grad,
    )


def solution(mesh):
    shard = ("samp", "tok")
    in_specs = (
        P("samp", "tok", None), P("samp", "tok", None), P(None, "tok", None), P(), P("samp"), P(),
        P(None, "tok", "samp", None), P(None, shard), P(shard), P(shard), P(shard, None), P(shard),
        P(shard, None), P(shard, None), P(shard, None), P(),
    )
    out_specs = (
        P("samp", "tok", None), P("samp", "tok", None), P(None, "tok", "samp"), P(None, "tok", "samp", None), P(),
        P(None, shard), P(shard), P(shard), P(shard, None), P(shard), P(shard, None), P(shard, None),
        P(shard, None), P(),
    )
    return jax.shard_map(per_device, mesh=mesh, in_specs=in_specs, out_specs=out_specs, check_vma=False)
```
